32 devices in a mesh: dp: 8 (over z, x), tensor: 4 (over y, core).
Axes of the slice: x: 2, y: 2, z: 4, core: 2. Of those that a mesh axis runs over, the one named last changes fastest.
Arguments:
- acts: bfloat16 [12288, 8192], P('dp', 'tensor'), may hold values from -60 to 60
- cotangent: bfloat16 [12288, 2048], P(('dp', 'tensor')), may hold values from -6 to 6
- master: float32 [8192, 2048], P('tensor', 'dp'), may hold values from -0.0625 to 0.0625
- first_moment: float32 [8192, 2048], P('tensor', 'dp'), may hold values from -4 to 4
- second_moment: float32 [8192, 2048], P('tensor', 'dp'), may hold values from 0.01 to 1
Outputs:
- new_master: float32 [8192, 2048], P('tensor', 'dp')
- new_first: float32 [8192, 2048], P('tensor', 'dp')
- new_second: float32 [8192, 2048], P('tensor', 'dp')
- weights: bfloat16 [8192, 2048], P('tensor')
- block_scales: float32 [64, 16], P('tensor')
The draws below stay inside these ranges and needn't reach their ends.
All inputs are finite; a program needn't handle non-finite values.
Results may differ from the reference program's by a relative error of at most 0.02.
Values may be sent and summed in bfloat16 or wider, within the bound.
No kernel may reach another device: no remote copies, remote signals or barrier semaphores. Data moves between devices by JAX's collectives and lax.ppermute only.
A program may use at most 192 MiB of HBM per device.

```python
import math
import jax
import jax.numpy as jnp
from jax import lax

D = 8192
BLOCK = 128
KV = 2048
TOKENS = 12288
N_DP = 8


def draw_acts(key, part):
    key = jax.random.fold_in(key, 11)
    first_key = jax.random.fold_in(key, 0)
    ramp = 1.0 + 2.0 * jnp.arange(TOKENS, dtype=jnp.float32) / TOKENS
    values = jnp.clip(jax.random.normal(first_key, (TOKENS, D), jnp.float32), -6.0, 6.0)
    return (values * ramp[:, None]).astype(jnp.bfloat16)


def level_of(key, extent, pieces, smallest, largest):
    loudness = 1.0
    for axis_at, blocks in pieces:
        heights = jax.random.uniform(jax.random.fold_in(jax.random.fold_in(key, 6), axis_at), (blocks,), jnp.float32, smallest / len(pieces), largest / len(pieces))
        loudness = loudness * jnp.repeat(jnp.exp(heights), extent[axis_at] // blocks).reshape((-1,) + (1,) * (len(extent) - 1 - axis_at))
    return loudness


def gaussian(own_key, shape, width, limit, cuts=(), held_as=jnp.bfloat16):
    factor_of = level_of(own_key, shape, cuts, -0.22, 0.18) if cuts else 1.0
    entries = jax.random.normal(own_key, shape, jnp.float32) * width * factor_of
    return jnp.minimum(jnp.maximum(entries, -limit), limit).astype(held_as)


def setup_inputs(seed: int = 0) -> dict:
    key_list = jax.random.split(jax.random.key(seed), 6)
    return {
        "acts": draw_acts(jax.random.fold_in(key_list[5], 71), 0),
        "cotangent": gaussian(key_list[1], (TOKENS, KV), 1.0, 6.0, ((0, 32),)),
        "master": gaussian(key_list[2], (D, KV), D ** -0.5, 0.0625, ((0, 4), (1, 8)), jnp.float32),
        "first_moment": gaussian(key_list[3], (D, KV), 0.5, 4.0, ((0, 4), (1, 8)), jnp.float32),
        "second_moment": jnp.clip(jnp.exp(math.log(1.0) - 4.6051702 * jax.random.uniform(key_list[4], (D, KV), jnp.float32) ** level_of(key_list[4], (D, KV), ((0, 4), (1, 8)), -0.2, 0.2)), 0.01, 1.0),
    }


def widen(small):
    return jnp.repeat(jnp.repeat(small, BLOCK, axis=0), BLOCK, axis=1)

def reference(acts, cotangent, master, first_moment, second_moment):
    groups_x = acts.reshape(N_DP, -1, D)
    groups_y = cotangent.reshape(N_DP, -1, KV)

    def one_group(pair):
        left, right = pair
        return lax.dot_general(left, right, (((0,), (0,)), ((), ())), preferred_element_type=jnp.float32)
    partial_value = lax.map(one_group, (groups_x, groups_y))
    magnitude = jnp.abs(partial_value).reshape(N_DP, D // BLOCK, BLOCK, KV // BLOCK, BLOCK)
    block_scales = lax.optimization_barrier(jnp.max(magnitude, axis=(0, 2, 4))) + 1e-06
    wide_scale = widen(block_scales)
    quantized = (partial_value / wide_scale[None]).astype(jnp.bfloat16)
    quantized = lax.optimization_barrier(quantized)
    summed = lax.optimization_barrier(jnp.sum(quantized.astype(jnp.float32), axis=0))
    gradient = summed * wide_scale / math.sqrt(TOKENS)
    new_first = 0.9 * first_moment + 0.1 * gradient
    new_second = 0.95 * second_moment + 0.05 * gradient * gradient
    first_hat = new_first / (1.0 - 0.9 ** 10)
    second_hat = new_second / (1.0 - 0.95 ** 10)
    new_master = master * (1.0 - 0.01 * 0.1) - 0.01 * first_hat / (jnp.sqrt(second_hat) + 1e-08)
    weights = new_master.astype(jnp.bfloat16)
    return (new_master, new_first, new_second, weights, block_scales)
```

```python
import math

import jax
import jax.numpy as jnp
from jax import lax
from jax.experimental import pallas as pl
from jax.experimental.pallas import tpu as pltpu
from jax.sharding import PartitionSpec as P

BLOCK = 128
Z = 4
F32 = jnp.float32
BF16 = jnp.bfloat16

ORDER = ((3, 2, 1, 0), (3, 2, 0, 1), (0, 1, 3, 2), (0, 1, 2, 3))
GATHER = ((0, 1, 2, 3), (1, 0, 2, 3), (2, 3, 1, 0), (3, 2, 1, 0))


def matmul_kernel(place_ref, acts_ref, *refs, parts, chunks, width):
    cot_refs, outs = refs[:parts], refs[parts : parts + chunks]
    max_ref, cot = refs[parts + chunks], refs[parts + chunks + 1]
    rows = cot_refs[0].shape[0]

    @pl.when(pl.program_id(0) == 0)
    def _():
        for k in range(parts):
            at = pl.multiple_of(place_ref[k] * rows, rows)
            cot[pl.ds(at, rows), :] = cot_refs[k][...]

    blocks = acts_ref.shape[0] // BLOCK
    for j in range(chunks):
        columns = slice(j * width, (j + 1) * width)
        acc = jnp.dot(acts_ref[...], cot[:, columns], preferred_element_type=F32)
        outs[j][...] = acc.astype(BF16)
        max_ref[0, :, columns] = jnp.max(jnp.abs(acc).reshape(blocks, BLOCK, width), axis=1)


def partial_chunks(place, acts_t, cot_parts, chunks):
    rows, tokens = acts_t.shape
    parts = len(cot_parts)
    part_rows, columns = cot_parts[0].shape
    width = columns // chunks
    step = 512
    blocks = step // BLOCK
    grid_spec = pltpu.PrefetchScalarGridSpec(
        num_scalar_prefetch=1,
        grid=(rows // step,),
        in_specs=[pl.BlockSpec((step, tokens), lambda i, p: (i, 0))]
        + [pl.BlockSpec((part_rows, columns), lambda i, p: (0, 0))] * parts,
        out_specs=[pl.BlockSpec((step, width), lambda i, p: (i, 0))] * chunks
        + [pl.BlockSpec((1, blocks, columns), lambda i, p: (i, 0, 0))],
        scratch_shapes=[pltpu.VMEM((tokens, columns), BF16)],
    )
    out = pl.pallas_call(
        lambda *refs: matmul_kernel(*refs, parts=parts, chunks=chunks, width=width),
        grid_spec=grid_spec,
        out_shape=[jax.ShapeDtypeStruct((rows, width), BF16)] * chunks
        + [jax.ShapeDtypeStruct((rows // step, blocks, columns), F32)],
        compiler_params=pltpu.CompilerParams(vmem_limit_bytes=40 * 1024 * 1024),
        cost_estimate=pl.CostEstimate(
            flops=2 * rows * tokens * columns,
            bytes_accessed=2 * (rows * tokens + tokens * columns + rows * columns),
            transcendentals=0,
        ),
        name="partials",
    )(place, acts_t, *cot_parts)
    maxima = out[chunks].reshape(rows // BLOCK, chunks, width // BLOCK, BLOCK).max(axis=3)
    return out[:chunks], maxima


def body(acts, cotangent, master, first_moment, second_moment):
    n_dp = lax.axis_size("dp")
    n_tensor = lax.axis_size("tensor")
    n_x = n_dp // Z
    owner = lax.axis_index("dp")
    z, x = owner // n_x, owner % n_x
    seat = lax.axis_index("tensor")
    rows, columns = acts.shape[1], cotangent.shape[1]
    width = columns // n_dp

    def z_perm(value, pairs):
        return lax.ppermute(value, "dp", [(a * n_x + i, b * n_x + i) for a, b in pairs for i in range(n_x)])

    def x_perm(value, by):
        return lax.ppermute(value, "dp", [(a * n_x + i, a * n_x + (i + by) % n_x) for a in range(Z) for i in range(n_x)])

    def seat_perm(value, flip):
        return lax.ppermute(value, "tensor", [(i, i ^ flip) for i in range(n_tensor)])

    def table(entries):
        return jnp.asarray(entries, jnp.int32)[z]

    order = [table([ORDER[a][i] for a in range(Z)]) for i in range(Z)]

    def column_of(slot, by):
        return (order[slot] * n_x + (x + by) % n_x) * width

    others = range(1, n_x)
    pieces = [
        [(0, by) for by in others],
        [(0, 0)] + [(1, by) for by in others],
        [(1, 0)] + [(2, by) for by in others] + [(2, 0)] + [(3, by) for by in others] + [(3, 0)],
    ]
    place = jnp.stack([seat ^ k for k in range(n_tensor)]).astype(jnp.int32)
    acts_t = lax.optimization_barrier(acts.T)

    partial, maxima, before = {}, {}, None
    for piece in pieces:
        own = jnp.concatenate(
            [lax.dynamic_slice_in_dim(cotangent, column_of(*at), width, 1) for at in piece], axis=1
        )
        if before is not None:
            own, before = lax.optimization_barrier((own, before))
        across = [own] + [seat_perm(own, k) for k in range(2, n_tensor, 2)]
        before = across[-1]
        cot_parts = [part for near in across for part in (near, seat_perm(near, 1))]
        chunks, block_max = partial_chunks(place, acts_t, cot_parts, len(piece))
        for j, at in enumerate(piece):
            partial[at] = chunks[j]
            maxima[at] = block_max[:, j]

    summed = []
    for i in range(Z):
        total = partial[i, 0].astype(F32)
        for by in others:
            total = total + x_perm(partial[i, by], by).astype(F32)
        summed.append(total)

    ends = (z == 0) | (z == Z - 1)
    first = z_perm(summed[0].astype(BF16), [(0, 1), (3, 2)])
    middle = jnp.where(ends, summed[1], summed[0] + first.astype(F32)).astype(BF16)
    up = z_perm(middle, [(0, 1), (1, 2)])
    down = z_perm(middle, [(3, 2), (2, 1)])
    up = z_perm((jnp.where(z == 1, summed[1], summed[2]) + up.astype(F32)).astype(BF16), [(0, 1), (1, 2), (2, 3)])
    down = z_perm((jnp.where(z == 2, summed[1], summed[2]) + down.astype(F32)).astype(BF16), [(3, 2), (2, 1), (1, 0)])
    total = summed[3] + up.astype(F32) + down.astype(F32)

    slots = [(i, by) for i in range(Z) for by in range(n_x)]
    scales = jnp.zeros((rows // BLOCK, columns // BLOCK), F32)
    for at in slots:
        scales = lax.dynamic_update_slice_in_dim(scales, maxima[at], column_of(*at) // BLOCK, 1)
    mine = scales
    for by in others:
        scales = jnp.maximum(scales, x_perm(mine, by))
    scales = jnp.maximum(scales, z_perm(scales, [(a, a ^ 1) for a in range(Z)]))
    scales = jnp.maximum(scales, z_perm(scales, [(a, a ^ 2) for a in range(Z)]))
    block_scales = scales + 1e-06

    gradient = total * (1.0 / math.sqrt(acts.shape[0] * n_dp))
    new_first = 0.9 * first_moment + 0.1 * gradient
    new_second = 0.95 * second_moment + 0.05 * gradient * gradient
    first_hat = new_first / (1.0 - 0.9**10)
    second_hat = new_second / (1.0 - 0.95**10)
    new_master = master * (1.0 - 0.01 * 0.1) - 0.01 * first_hat / (jnp.sqrt(second_hat) + 1e-08)
    owned = new_master.astype(BF16)

    up1 = z_perm(owned, [(0, 1), (1, 2), (2, 3)])
    down1 = z_perm(owned, [(3, 2), (2, 1), (1, 0)])
    up2 = z_perm(up1, [(1, 2), (2, 3)])
    down2 = z_perm(down1, [(2, 1), (1, 0)])
    far2 = jnp.where(z >= 2, up2, down2)
    far3 = z_perm(far2, [(2, 3), (1, 0)])
    held = [
        owned,
        jnp.where(z % 2 == 1, up1, down1),
        jnp.where(ends, far2, jnp.where(z == 1, down1, up1)),
        jnp.where(ends, far3, far2),
    ]
    weights = jnp.zeros((rows, columns), BF16)
    for i in range(Z):
        at = table([GATHER[a][i] for a in range(Z)])
        weights = lax.dynamic_update_slice_in_dim(weights, held[i], (at * n_x + x) * width, 1)
        for by in others:
            got = x_perm(held[i], by)
            weights = lax.dynamic_update_slice_in_dim(weights, got, (at * n_x + (x - by) % n_x) * width, 1)
    return (new_master, new_first, new_second, weights, block_scales)


def solution(mesh):
    in_specs = (
        P("dp", "tensor"),
        P(("dp", "tensor"), None),
        P("tensor", "dp"),
        P("tensor", "dp"),
        P("tensor", "dp"),
    )
    out_specs = (
        P("tensor", "dp"),
        P("tensor", "dp"),
        P("tensor", "dp"),
        P("tensor", None),
        P("tensor", None),
    )
    return jax.shard_map(body, mesh=mesh, in_specs=in_specs, out_specs=out_specs, check_vma=False)
```

```python
import math

import jax
import jax.numpy as jnp
from jax import lax
from jax.experimental import pallas as pl
from jax.experimental.pallas import tpu as pltpu
from jax.sharding import PartitionSpec as P

BLOCK = 128
Z = 4
F32 = jnp.float32
BF16 = jnp.bfloat16
VMEM = pl.BlockSpec(memory_space=pltpu.VMEM)
FREE = pl.CostEstimate(flops=0, bytes_accessed=0, transcendentals=0)

INWARDS = ((0, 1), (3, 2))
OUTWARDS = ((1, 0), (2, 3))
MIDDLE = ((1, 2), (2, 1))
PAIRS = ((0, 1), (1, 0), (2, 3), (3, 2))


def owner_z(z, slot):
    low = z < 2
    if slot == 3:
        return z
    if slot == 0:
        return jnp.where(low, 3, 0)
    end = (z == 0) | (z == Z - 1)
    two, one = jnp.where(low, 2, 1), jnp.where(end, jnp.where(low, 1, 2), jnp.where(low, 0, 3))
    return two if slot == 1 else one


def call(kernel, out_shape, operands, name):
    return pl.pallas_call(
        kernel,
        out_shape=list(out_shape),
        in_specs=[VMEM] * len(operands),
        out_specs=[VMEM] * len(out_shape),
        cost_estimate=FREE,
        name=name,
    )


def arrange(cot, pieces, width, n_x):
    def kernel(cot_ref, *outs):
        owner = lax.axis_index("dp")
        z, x = owner // n_x, owner % n_x
        for piece, out in zip(pieces, outs):
            for j, (slot, by) in enumerate(piece):
                at = pl.multiple_of((owner_z(z, slot) * n_x + (x + by) % n_x) * width, width)
                out[:, j * width : (j + 1) * width] = cot_ref[:, pl.ds(at, width)]

    shapes = [jax.ShapeDtypeStruct((cot.shape[0], len(piece) * width), BF16) for piece in pieces]
    return call(kernel, shapes, [cot], "arrange")(cot)


def multiply(acts_t, group, chunks, width):
    rows, tokens = acts_t.shape
    depth, columns = group[0].shape
    step = min(rows, 512)
    blocks = step // BLOCK

    def kernel(acts_ref, *refs):
        parts, outs, top, cot = refs[: len(group)], refs[len(group) : -2], refs[-2], refs[-1]

        @pl.when(pl.program_id(0) == 0)
        def _():
            seat = lax.axis_index("tensor")
            for k, part in enumerate(parts):
                cot[pl.ds(pl.multiple_of((seat ^ k) * depth, depth), depth), :] = part[...]

        for j, out in enumerate(outs):
            here = slice(j * width, (j + 1) * width)
            acc = jnp.dot(acts_ref[...], cot[:, here], preferred_element_type=F32)
            out[...] = acc.astype(BF16)
            top[0, :, here] = jnp.max(jnp.abs(acc).reshape(blocks, BLOCK, width), axis=1)

    out = pl.pallas_call(
        kernel,
        grid=(rows // step,),
        in_specs=[pl.BlockSpec((step, tokens), lambda i: (i, 0))]
        + [pl.BlockSpec((depth, columns), lambda i: (0, 0))] * len(group),
        out_specs=[pl.BlockSpec((step, width), lambda i: (i, 0))] * chunks
        + [pl.BlockSpec((1, blocks, columns), lambda i: (i, 0, 0))],
        out_shape=[jax.ShapeDtypeStruct((rows, width), BF16)] * chunks
        + [jax.ShapeDtypeStruct((rows // step, blocks, columns), F32)],
        scratch_shapes=[pltpu.VMEM((tokens, columns), BF16)],
        compiler_params=pltpu.CompilerParams(vmem_limit_bytes=48 * 1024 * 1024),
        cost_estimate=FREE,
        name="partials",
    )(acts_t, *group)
    return out[:chunks], out[chunks]


def add(terms):
    rows, columns = terms[0].shape
    step = 64

    def kernel(*refs):
        def one(i, carry):
            here = pl.ds(pl.multiple_of(i * step, step), step)
            total = refs[0][here, :].astype(F32)
            for ref in refs[1:-1]:
                total = total + ref[here, :].astype(F32)
            refs[-1][here, :] = total.astype(BF16)
            return carry

        lax.fori_loop(0, rows // step, one, 0, unroll=4)

    return call(kernel, [jax.ShapeDtypeStruct((rows, columns), BF16)], terms, "add")(*terms)[0]


def adamw(terms, states, factor):
    rows, width = states[0].shape
    rate = 0.01 / (1.0 - 0.9**10)
    spread = 1.0 / (1.0 - 0.95**10)
    step = 64

    def kernel(*refs):
        master_ref, first_ref, second_ref, new_master_ref, new_first_ref, new_second_ref, weights_ref = refs[len(terms) :]

        def one(i, carry):
            at = pl.ds(pl.multiple_of(i * step, step), step)
            total = refs[0][at, :].astype(F32)
            for ref in refs[1 : len(terms)]:
                total = total + ref[at, :].astype(F32)
            gradient = total * factor
            new_first = 0.9 * first_ref[at, :] + 0.1 * gradient
            new_second = 0.95 * second_ref[at, :] + (0.05 * gradient) * gradient
            hat = new_second * spread
            root = hat * lax.rsqrt(hat) + 1e-08
            inverse = pl.reciprocal(root, approx=True)
            inverse = inverse * (2.0 - root * inverse)
            new_master = master_ref[at, :] * (1.0 - 0.01 * 0.1) - (rate * new_first) * inverse
            new_master_ref[at, :] = new_master
            new_first_ref[at, :] = new_first
            new_second_ref[at, :] = new_second
            weights_ref[at, :] = new_master.astype(BF16)
            return carry

        lax.fori_loop(0, rows // step, one, 0, unroll=2)

    shapes = [jax.ShapeDtypeStruct((rows, width), F32)] * 3 + [jax.ShapeDtypeStruct((rows, width), BF16)]
    return call(kernel, shapes, list(terms) + list(states), "adamw")(*terms, *states)


def blank(shape, dtype):
    return pl.pallas_call(
        lambda ref: None,
        out_specs=pl.BlockSpec(memory_space=pl.ANY),
        out_shape=jax.ShapeDtypeStruct(shape, dtype),
        cost_estimate=FREE,
        name="blank",
    )()


def after(value, *earlier):
    return lax.optimization_barrier((value, *earlier))[0] if earlier else value


def body(acts, cotangent, master, first_moment, second_moment):
    n_dp = lax.axis_size("dp")
    n_tensor = lax.axis_size("tensor")
    n_x = n_dp // Z
    owner = lax.axis_index("dp")
    z, x = owner // n_x, owner % n_x
    rows, columns = acts.shape[1], cotangent.shape[1]
    width = columns // n_dp
    high = width // BLOCK
    others = range(1, n_x)

    def z_perm(value, pairs):
        return lax.ppermute(value, "dp", [(a * n_x + i, b * n_x + i) for a, b in pairs for i in range(n_x)])

    def x_perm(value, by, where=range(Z)):
        pairs = [(a * n_x + i, a * n_x + (i + by) % n_x) for a in where for i in range(n_x)]
        return lax.ppermute(value, "dp", pairs)

    def seat_perm(value, flip):
        return lax.ppermute(value, "tensor", [(i, i ^ flip) for i in range(n_tensor)])

    pieces = [[(0, by) for by in others]]
    pieces += [[(i, 0)] + [(i + 1, by) for by in others] for i in range(Z - 1)]
    pieces[-1].append((Z - 1, 0))
    own = arrange(cotangent, pieces, width, n_x)
    partial, tops, across = {}, [], []

    def fetch(piece, *earlier):
        value = after(own[piece], *earlier)
        across.append([value] + [seat_perm(value, k) for k in range(2, n_tensor, 2)])

    def partials(piece, *earlier):
        group = [part for value in across[piece] for part in (value, seat_perm(after(value, *earlier), 1))]
        chunks, top = multiply(after(acts_t, *earlier), group, len(pieces[piece]), width)
        partial.update(zip(pieces[piece], chunks))
        tops.append(top)
        return chunks[0]

    def send_x(slot, *earlier):
        return [x_perm(after(partial[slot, by], *earlier), by) for by in others]

    fetch(0)
    acts_t = after(acts, own[0]).T
    token = partials(0, acts_t)
    got0 = send_x(0)
    fetch(1, token)
    token = partials(1, token)
    fetch(2, token)
    got1 = send_x(1, *got0)
    sum0 = add([after(partial[0, 0], token), *got0])
    far = z_perm(sum0, INWARDS)
    token = partials(2, sum0)
    fetch(3, token)
    got2 = send_x(2, *got1, token)
    sum1 = add([after(partial[1, 0], token), *got1])
    inwards = z_perm(sum1, INWARDS)
    sum0 = add([after(partial[0, 0], sum1), *got0, far])
    middle = z_perm(sum0, MIDDLE)
    token = partials(3, sum0)

    top = jnp.concatenate([after(t, token).reshape(rows // BLOCK, -1, BLOCK).max(axis=2) for t in tops], axis=1)
    column = jnp.stack(
        [(owner_z(z, i) * n_x + (x + by) % n_x) * high + h for piece in pieces for i, by in piece for h in range(high)]
    )
    here = column[None, :, None] == jnp.arange(n_dp * high)[None, None, :]
    scales = jnp.max(jnp.where(here, top[:, :, None], 0.0), axis=1)
    scales_x = [x_perm(scales, by) for by in others]

    got3 = send_x(3, *got2, scales)
    for got in scales_x:
        scales = jnp.maximum(scales, got)
    sum2 = add([after(partial[2, 0], scales), *got2, middle])
    pairs = z_perm(sum2, PAIRS)
    sum1 = add([after(partial[1, 0], sum2), *got1, inwards])
    last = z_perm(sum1, MIDDLE)
    scales_z = z_perm(after(scales, sum1), PAIRS)

    scales = jnp.maximum(scales, scales_z)
    new_master, new_first, new_second, owned = adamw(
        [after(partial[3, 0], scales), *got3, pairs, last],
        [master, first_moment, second_moment],
        1.0 / math.sqrt(acts.shape[0] * n_dp),
    )

    weights = blank((rows, columns), BF16)
    low, between = z < 2, (z == 1) | (z == 2)
    sources = [z, z ^ 1, jnp.where(low, 2, 1), jnp.where(low, 3, 0)]
    over0 = [[x_perm(owned, by)] for by in others]
    pairs, mid = z_perm(owned, PAIRS), z_perm(owned, MIDDLE)
    scales_z = z_perm(after(scales, owned), [(a, a ^ 2) for a in range(Z)])
    block_scales = jnp.maximum(scales, scales_z) + 1e-06
    over1 = [[x_perm(after(pairs, *(v for vs in over0 for v in vs)), by)] for by in others]
    outwards, mid_far = z_perm(after(mid, block_scales), OUTWARDS), z_perm(after(pairs, block_scales), MIDDLE)
    before = [v for vs in over1 for v in vs]
    over2 = [[x_perm(after(mid, *before), by, (1, 2)), x_perm(after(outwards, *before), by, (0, 3))] for by in others]
    far = z_perm(mid_far, OUTWARDS)
    before = [v for vs in over2 for v in vs]
    over3 = [[x_perm(after(mid_far, *before), by, (1, 2)), x_perm(after(far, *before), by, (0, 3))] for by in others]

    def put(weights, values, slot, by):
        value = values[0] if len(values) == 1 else jnp.where(between, *values)
        return lax.dynamic_update_slice(weights, value, (0, (sources[slot] * n_x + (x - by) % n_x) * width))

    held = [owned], [pairs], [mid, outwards], [mid_far, far]
    for slot, over in enumerate([over0, over1, over2, over3]):
        weights = put(weights, held[slot], slot, 0)
        for by in others:
            weights = put(weights, over[by - 1], slot, by)
    return (new_master, new_first, new_second, weights, block_scales)


def solution(mesh):
    in_specs = (
        P("dp", "tensor"),
        P(("dp", "tensor"), None),
        P("tensor", "dp"),
        P("tensor", "dp"),
        P("tensor", "dp"),
    )
    out_specs = (
        P("tensor", "dp"),
        P("tensor", "dp"),
        P("tensor", "dp"),
        P("tensor", None),
        P("tensor", None),
    )
    return jax.shard_map(body, mesh=mesh, in_specs=in_specs, out_specs=out_specs, check_vma=False)
```

```python
import math

import jax
import jax.numpy as jnp
from jax import lax
from jax.experimental import pallas as pl
from jax.experimental.pallas import tpu as pltpu
from jax.sharding import PartitionSpec as P

BLOCK = 128
Z = 4
F32 = jnp.float32
BF16 = jnp.bfloat16
VMEM = pl.BlockSpec(memory_space=pltpu.VMEM)
FREE = pl.CostEstimate(flops=0, bytes_accessed=0, transcendentals=0)

INWARDS = ((0, 1), (3, 2))
OUTWARDS = ((1, 0), (2, 3))
MIDDLE = ((1, 2), (2, 1))
PAIRS = ((0, 1), (1, 0), (2, 3), (3, 2))


def owner_z(z, slot):
    low = z < 2
    if slot == 3:
        return z
    if slot == 0:
        return jnp.where(low, 3, 0)
    end = (z == 0) | (z == Z - 1)
    two, one = jnp.where(low, 2, 1), jnp.where(end, jnp.where(low, 1, 2), jnp.where(low, 0, 3))
    return two if slot == 1 else one


def call(kernel, out_shape, operands, name):
    return pl.pallas_call(
        kernel,
        out_shape=list(out_shape),
        in_specs=[VMEM] * len(operands),
        out_specs=[VMEM] * len(out_shape),
        cost_estimate=FREE,
        name=name,
    )


def arrange(cot, pieces, width, n_x):
    def kernel(cot_ref, *outs):
        owner = lax.axis_index("dp")
        z, x = owner // n_x, owner % n_x
        for piece, out in zip(pieces, outs):
            for j, (slot, by) in enumerate(piece):
                at = pl.multiple_of((owner_z(z, slot) * n_x + (x + by) % n_x) * width, width)
                out[:, j * width : (j + 1) * width] = cot_ref[:, pl.ds(at, width)]

    shapes = [jax.ShapeDtypeStruct((cot.shape[0], len(piece) * width), BF16) for piece in pieces]
    return call(kernel, shapes, [cot], "arrange")(cot)


def multiply(acts_t, group, chunks, width):
    rows, tokens = acts_t.shape
    depth, columns = group[0].shape
    step = min(rows, 512)
    blocks = step // BLOCK

    def kernel(acts_ref, *refs):
        parts, outs, top, cot = refs[: len(group)], refs[len(group) : -2], refs[-2], refs[-1]

        @pl.when(pl.program_id(0) == 0)
        def _():
            seat = lax.axis_index("tensor")
            for k, part in enumerate(parts):
                cot[pl.ds(pl.multiple_of((seat ^ k) * depth, depth), depth), :] = part[...]

        for j, out in enumerate(outs):
            here = slice(j * width, (j + 1) * width)
            acc = jnp.dot(acts_ref[...], cot[:, here], preferred_element_type=F32)
            out[...] = acc.astype(BF16)
            top[0, :, here] = jnp.max(jnp.abs(acc).reshape(blocks, BLOCK, width), axis=1)

    out = pl.pallas_call(
        kernel,
        grid=(rows // step,),
        in_specs=[pl.BlockSpec((step, tokens), lambda i: (i, 0))]
        + [pl.BlockSpec((depth, columns), lambda i: (0, 0))] * len(group),
        out_specs=[pl.BlockSpec((step, width), lambda i: (i, 0))] * chunks
        + [pl.BlockSpec((1, blocks, columns), lambda i: (i, 0, 0))],
        out_shape=[jax.ShapeDtypeStruct((rows, width), BF16)] * chunks
        + [jax.ShapeDtypeStruct((rows // step, blocks, columns), F32)],
        scratch_shapes=[pltpu.VMEM((tokens, columns), BF16)],
        compiler_params=pltpu.CompilerParams(vmem_limit_bytes=48 * 1024 * 1024),
        cost_estimate=FREE,
        name="partials",
    )(acts_t, *group)
    return out[:chunks], out[chunks]


def add(terms, *earlier):
    held = lax.optimization_barrier((*terms, *earlier))[: len(terms)]
    total = held[0].astype(F32)
    for term in held[1:]:
        total = total + term.astype(F32)
    return lax.optimization_barrier(total.astype(BF16))


def adamw(terms, states, factor, first, count):
    total, *rest = [lax.slice_in_dim(term, first, first + count).astype(F32) for term in terms]
    for term in rest:
        total = total + term
    master, first_moment, second_moment = [lax.slice_in_dim(state, first, first + count) for state in states]
    gradient = total * factor
    new_first = 0.9 * first_moment + 0.1 * gradient
    new_second = 0.95 * second_moment + 0.05 * gradient * gradient
    first_hat = new_first * (1.0 / (1.0 - 0.9**10))
    second_hat = new_second * (1.0 / (1.0 - 0.95**10))
    new_master = master * (1.0 - 0.01 * 0.1) - 0.01 * first_hat / (jnp.sqrt(second_hat) + 1e-08)
    return new_master, new_first, new_second, new_master.astype(BF16)


def blank(shape, dtype):
    return pl.pallas_call(
        lambda ref: None,
        out_specs=pl.BlockSpec(memory_space=pl.ANY),
        out_shape=jax.ShapeDtypeStruct(shape, dtype),
        cost_estimate=FREE,
        name="blank",
    )()


def after(value, *earlier):
    return lax.optimization_barrier((value, *earlier))[0] if earlier else value


def body(acts, cotangent, master, first_moment, second_moment):
    n_dp = lax.axis_size("dp")
    n_tensor = lax.axis_size("tensor")
    n_x = n_dp // Z
    owner = lax.axis_index("dp")
    z, x = owner // n_x, owner % n_x
    rows, columns = acts.shape[1], cotangent.shape[1]
    width = columns // n_dp
    high = width // BLOCK
    others = range(1, n_x)

    def z_perm(value, pairs):
        return lax.ppermute(value, "dp", [(a * n_x + i, b * n_x + i) for a, b in pairs for i in range(n_x)])

    def x_perm(value, by, where=range(Z)):
        pairs = [(a * n_x + i, a * n_x + (i + by) % n_x) for a in where for i in range(n_x)]
        return lax.ppermute(value, "dp", pairs)

    def seat_perm(value, flip):
        return lax.ppermute(value, "tensor", [(i, i ^ flip) for i in range(n_tensor)])

    pieces = [
        [(0, by) for by in others],
        [(0, 0)] + [(1, by) for by in others],
        [(1, 0)] + [(i, by) for i in (2, 3) for by in others],
        [(2, 0), (3, 0)],
    ]
    own = arrange(cotangent, pieces, width, n_x)
    partial, tops, across = {}, [], []

    def fetch(piece, *earlier):
        value = after(own[piece], *earlier)
        across.append([value] + [seat_perm(value, k) for k in range(2, n_tensor, 2)])

    def partials(piece, *earlier):
        group = [part for value in across[piece] for part in (value, seat_perm(after(value, *earlier), 1))]
        chunks, top = multiply(after(acts_t, *earlier), group, len(pieces[piece]), width)
        partial.update(zip(pieces[piece], chunks))
        tops.append(top)
        return chunks[0]

    def send_x(slot, *earlier):
        return [x_perm(after(partial[slot, by], *earlier), by) for by in others]

    fetch(0)
    acts_t = after(acts, own[0]).T
    token = partials(0, acts_t)
    got0 = send_x(0)
    fetch(1, token)
    token = partials(1, token)
    got1 = send_x(1)
    fetch(2, across[1][-1])
    sum0 = add([partial[0, 0], *got0], token)
    far = z_perm(sum0, INWARDS)
    token = partials(2, sum0)
    got2, got3 = send_x(2), send_x(3)
    fetch(3, across[2][-1], sum0)
    token = partials(3, token)
    sum1 = add([partial[1, 0], *got1], token)
    inwards = z_perm(sum1, INWARDS)
    sum0 = add([partial[0, 0], *got0, far], sum1)
    middle = z_perm(sum0, MIDDLE)

    top = jnp.concatenate([after(t, sum0).reshape(rows // BLOCK, -1, BLOCK).max(axis=2) for t in tops], axis=1)
    column = jnp.stack(
        [(owner_z(z, i) * n_x + (x + by) % n_x) * high + h for piece in pieces for i, by in piece for h in range(high)]
    )
    here = column[None, :, None] == jnp.arange(n_dp * high)[None, None, :]
    scales = jnp.max(jnp.where(here, top[:, :, None], 0.0), axis=1)
    scales_x = [x_perm(scales, by) for by in others]

    sum1 = add([partial[1, 0], *got1, inwards], scales)
    last = z_perm(sum1, MIDDLE)
    sum2 = add([partial[2, 0], *got2, middle], sum1)
    pairs = z_perm(sum2, PAIRS)
    scales = after(scales, sum2)
    for got in scales_x:
        scales = jnp.maximum(scales, got)
    scales_z = z_perm(scales, PAIRS)

    terms = [partial[3, 0], *got3, last, pairs]
    states = [master, first_moment, second_moment]
    factor = 1.0 / math.sqrt(acts.shape[0] * n_dp)
    half = rows // 2
    scales = jnp.maximum(scales, scales_z)
    owned, token = [], scales
    for h in range(2):
        held = lax.optimization_barrier((*terms, *states, token))
        token = lax.optimization_barrier(adamw(held[: len(terms)], held[len(terms) : -1], factor, h * half, half)[3])
        owned.append(token)
    held = lax.optimization_barrier((*terms, *states, token))
    new_master, new_first, new_second, _ = adamw(held[: len(terms)], held[len(terms) : -1], factor, 0, rows)

    weights = blank((rows, columns), BF16)
    low, between = z < 2, (z == 1) | (z == 2)
    sources = [z, z ^ 1, jnp.where(low, 2, 1), jnp.where(low, 3, 0)]

    def over_x(value, where=range(Z)):
        return [x_perm(value, by, where) for by in others]

    over0 = [over_x(value) for value in owned]
    pairs = [z_perm(value, PAIRS) for value in owned]
    mid = [z_perm(value, MIDDLE) for value in owned]
    mid_far = [z_perm(value, MIDDLE) for value in pairs]
    outwards = [z_perm(value, OUTWARDS) for value in mid]
    over1 = [over_x(value) for value in pairs]
    over_mid = [over_x(value, (1, 2)) for value in mid]
    far = [z_perm(mid_far[0], OUTWARDS), z_perm(mid_far[1], OUTWARDS)]
    over_outwards = [over_x(value, (0, 3)) for value in outwards]
    over_mid_far = [over_x(value, (1, 2)) for value in mid_far]
    over_far = [over_x(value, (0, 3)) for value in far]
    scales_z = z_perm(after(scales, owned[0]), [(a, a ^ 2) for a in range(Z)])
    block_scales = jnp.maximum(scales, scales_z) + 1e-06

    def put(weights, h, slot, by, *values):
        value = values[0] if len(values) == 1 else jnp.where(between, *values)
        at = (sources[slot] * n_x + (x - by) % n_x) * width
        return lax.dynamic_update_slice(weights, value, (h * half, at))

    for slot, held in enumerate([(owned,), (pairs,), (mid, outwards), (mid_far, far)]):
        over = [(over0,), (over1,), (over_mid, over_outwards), (over_mid_far, over_far)][slot]
        for h in range(2):
            weights = put(weights, h, slot, 0, *[value[h] for value in held])
        for h in range(2):
            for by in others:
                weights = put(weights, h, slot, by, *[value[h][by - 1] for value in over])
    return (new_master, new_first, new_second, weights, block_scales)


def solution(mesh):
    in_specs = (
        P("dp", "tensor"),
        P(("dp", "tensor"), None),
        P("tensor", "dp"),
        P("tensor", "dp"),
        P("tensor", "dp"),
    )
    out_specs = (
        P("tensor", "dp"),
        P("tensor", "dp"),
        P("tensor", "dp"),
        P("tensor", None),
        P("tensor", None),
    )
    return jax.shard_map(body, mesh=mesh, in_specs=in_specs, out_specs=out_specs, check_vma=False)
```

```python
import math

import jax
import jax.numpy as jnp
from jax import lax
from jax.experimental import pallas as pl
from jax.experimental.pallas import tpu as pltpu
from jax.sharding import PartitionSpec as P

BLOCK = 128
Z = 4
F32 = jnp.float32
BF16 = jnp.bfloat16
VMEM = pl.BlockSpec(memory_space=pltpu.VMEM)
FREE = pl.CostEstimate(flops=0, bytes_accessed=0, transcendentals=0)

INWARDS = ((0, 1), (3, 2))
OUTWARDS = ((1, 0), (2, 3))
MIDDLE = ((1, 2), (2, 1))
PAIRS = ((0, 1), (1, 0), (2, 3), (3, 2))


def owner_z(z, slot):
    low = z < 2
    if slot == 3:
        return z
    if slot == 0:
        return jnp.where(low, 3, 0)
    end = (z == 0) | (z == Z - 1)
    two, one = jnp.where(low, 2, 1), jnp.where(end, jnp.where(low, 1, 2), jnp.where(low, 0, 3))
    return two if slot == 1 else one


def call(kernel, out_shape, operands, name):
    return pl.pallas_call(
        kernel,
        out_shape=list(out_shape),
        in_specs=[VMEM] * len(operands),
        out_specs=[VMEM] * len(out_shape),
        cost_estimate=FREE,
        name=name,
    )


def arrange(cot, pieces, width, n_x):
    def kernel(cot_ref, *outs):
        owner = lax.axis_index("dp")
        z, x = owner // n_x, owner % n_x
        for piece, out in zip(pieces, outs):
            for j, (slot, by) in enumerate(piece):
                at = pl.multiple_of((owner_z(z, slot) * n_x + (x + by) % n_x) * width, width)
                out[:, j * width : (j + 1) * width] = cot_ref[:, pl.ds(at, width)]

    shapes = [jax.ShapeDtypeStruct((cot.shape[0], len(piece) * width), BF16) for piece in pieces]
    return call(kernel, shapes, [cot], "arrange")(cot)


def multiply(acts_t, group, chunks, width, cost):
    rows, tokens = acts_t.shape
    depth, columns = group[0].shape
    step = min(rows, 512)
    blocks = step // BLOCK

    def kernel(acts_ref, *refs):
        parts, outs, top, cot = refs[: len(group)], refs[len(group) : -2], refs[-2], refs[-1]

        @pl.when(pl.program_id(0) == 0)
        def _():
            seat = lax.axis_index("tensor")
            for k, part in enumerate(parts):
                cot[pl.ds(pl.multiple_of((seat ^ k) * depth, depth), depth), :] = part[...]

        for j in range(chunks):
            here = slice(j * width, (j + 1) * width)
            acc = jnp.dot(acts_ref[...], cot[:, here], preferred_element_type=F32)
            top[0, :, here] = jnp.max(jnp.abs(acc).reshape(blocks, BLOCK, width), axis=1)
            outs[j][...] = acc.astype(BF16)

    out = pl.pallas_call(
        kernel,
        grid=(rows // step,),
        in_specs=[pl.BlockSpec((step, tokens), lambda i: (i, 0))]
        + [pl.BlockSpec((depth, columns), lambda i: (0, 0))] * len(group),
        out_specs=[pl.BlockSpec((step, width), lambda i: (i, 0))] * chunks
        + [pl.BlockSpec((1, blocks, columns), lambda i: (i, 0, 0))],
        out_shape=[jax.ShapeDtypeStruct((rows, width), BF16)] * chunks
        + [jax.ShapeDtypeStruct((rows // step, blocks, columns), F32)],
        scratch_shapes=[pltpu.VMEM((tokens, columns), BF16)],
        compiler_params=pltpu.CompilerParams(vmem_limit_bytes=48 * 1024 * 1024),
        cost_estimate=cost,
        name="partials",
    )(acts_t, *group)
    return out[:chunks], out[chunks]


def add(terms, *earlier, rows=None):
    held = lax.optimization_barrier((*terms, *earlier))[: len(terms)]
    if rows is not None:
        held = [term if term.shape[0] == rows[1] else lax.slice_in_dim(term, rows[0], sum(rows)) for term in held]
    total = held[0].astype(F32)
    for term in held[1:]:
        total = total + term.astype(F32)
    return lax.optimization_barrier(total.astype(BF16))


def adamw(terms, states, factor):
    total = terms[0].astype(F32)
    for term in terms[1:]:
        total = total + term.astype(F32)
    master, first_moment, second_moment = states
    gradient = total * factor
    new_first = 0.9 * first_moment + 0.1 * gradient
    new_second = 0.95 * second_moment + 0.05 * gradient * gradient
    first_hat = new_first * (1.0 / (1.0 - 0.9**10))
    second_hat = new_second * (1.0 / (1.0 - 0.95**10))
    new_master = master * (1.0 - 0.01 * 0.1) - 0.01 * first_hat / (jnp.sqrt(second_hat) + 1e-08)
    return new_master, new_first, new_second, new_master.astype(BF16)


def update(terms, states, factor, wanted, name):
    rows, width = states[0].shape
    step = min(rows // 2, 512)
    half = rows // 2 // step
    flat = [value for term in terms for value in (term if isinstance(term, tuple) else (term,))]
    dtypes = [(F32, F32, F32, BF16)[k] for k in wanted]

    def kernel(*refs):
        ins, outs = refs[: len(flat) + 3], refs[len(flat) + 3 :]
        values, at = [], 0
        for term in terms:
            if isinstance(term, tuple):
                values.append(jnp.where(pl.program_id(0) < half, ins[at][...], ins[at + 1][...]))
                at += 2
            else:
                values.append(ins[at][...])
                at += 1
        results = adamw(values, [ref[...] for ref in ins[at:]], factor)
        for out, k in zip(outs, wanted):
            out[...] = results[k]

    whole = pl.BlockSpec((step, width), lambda i: (i, 0))
    halves = [
        pl.BlockSpec((step, width), lambda i: (jnp.minimum(i, half - 1), 0)),
        pl.BlockSpec((step, width), lambda i: (jnp.maximum(i - half, 0), 0)),
    ]
    specs = [spec for term in terms for spec in (halves if isinstance(term, tuple) else [whole])]
    return pl.pallas_call(
        kernel,
        grid=(rows // step,),
        in_specs=specs + [whole] * 3,
        out_specs=[whole] * len(wanted),
        out_shape=[jax.ShapeDtypeStruct((rows, width), dtype) for dtype in dtypes],
        compiler_params=pltpu.CompilerParams(vmem_limit_bytes=48 * 1024 * 1024),
        cost_estimate=FREE,
        name=name,
    )(*flat, *states)


def blank(shape, dtype):
    return pl.pallas_call(
        lambda ref: None,
        out_specs=pl.BlockSpec(memory_space=pl.ANY),
        out_shape=jax.ShapeDtypeStruct(shape, dtype),
        cost_estimate=FREE,
        name="blank",
    )()


def after(value, *earlier):
    return lax.optimization_barrier((value, *earlier))[0] if earlier else value


def body(acts, cotangent, master, first_moment, second_moment):
    n_dp = lax.axis_size("dp")
    n_tensor = lax.axis_size("tensor")
    n_x = n_dp // Z
    owner = lax.axis_index("dp")
    z, x = owner // n_x, owner % n_x
    rows, columns = acts.shape[1], cotangent.shape[1]
    width = columns // n_dp
    high = width // BLOCK
    others = range(1, n_x)

    def z_perm(value, pairs):
        return lax.ppermute(value, "dp", [(a * n_x + i, b * n_x + i) for a, b in pairs for i in range(n_x)])

    def x_perm(value, by, where=range(Z)):
        pairs = [(a * n_x + i, a * n_x + (i + by) % n_x) for a in where for i in range(n_x)]
        return lax.ppermute(value, "dp", pairs)

    def seat_perm(value, flip):
        return lax.ppermute(value, "tensor", [(i, i ^ flip) for i in range(n_tensor)])

    pieces = [
        [(0, by) for by in others],
        [(0, 0)] + [(1, by) for by in others],
        [(i, by) for i in (2, 3) for by in others] + [(1, 0), (2, 0), (3, 0)],
    ]
    own = arrange(cotangent, pieces, width, n_x)
    partial, tops, across = {}, [], []

    def fetch(piece, *earlier):
        value = after(own[piece], *earlier)
        across.append([value] + [seat_perm(value, k) for k in range(2, n_tensor, 2)])

    def partials(piece, *earlier):
        group = [part for value in across[piece] for part in (value, seat_perm(after(value, *earlier), 1))]
        cost = FREE if piece else pl.CostEstimate(flops=10**10, bytes_accessed=acts.size, transcendentals=0)
        chunks, top = multiply(after(acts_t, *earlier), group, len(pieces[piece]), width, cost)
        partial.update(zip(pieces[piece], chunks))
        tops.append(top)
        return chunks[0]

    def send_x(slot):
        return [x_perm(partial[slot, by], by) for by in others]

    half = rows // 2
    halves = range(2)
    part = [(h * half, half) for h in halves]

    for piece in range(len(pieces)):
        fetch(piece)
    acts_t = after(acts, *own).T
    token = partials(0, acts_t)
    got0 = send_x(0)
    token = partials(1, token)
    got1 = send_x(1)
    far, middle = [None] * 2, [None] * 2
    for h in halves:
        token = add([partial[0, 0], *got0], token, rows=part[h])
        far[h] = z_perm(token, INWARDS)
    token = partials(2, token)
    got2, got3 = send_x(2), send_x(3)
    token = add([partial[1, 0], *got1], token)
    inwards = z_perm(token, INWARDS)
    for h in halves:
        token = add([partial[0, 0], *got0, far[h]], token, rows=part[h])
        middle[h] = z_perm(token, MIDDLE)

    top = jnp.concatenate([after(t, token).reshape(rows // BLOCK, -1, BLOCK).max(axis=2) for t in tops], axis=1)
    column = jnp.stack(
        [(owner_z(z, i) * n_x + (x + by) % n_x) * high + h for piece in pieces for i, by in piece for h in range(high)]
    )
    here = column[None, :, None] == jnp.arange(n_dp * high)[None, None, :]
    scales = jnp.max(jnp.where(here, top[:, :, None], 0.0), axis=1)
    scales_x = [x_perm(scales, by) for by in others]

    pairs = [None] * 2
    token = add([partial[2, 0], *got2, middle[0]], scales, rows=part[0])
    pairs[0] = z_perm(token, PAIRS)
    token = add([partial[1, 0], *got1, inwards], token)
    last = z_perm(token, MIDDLE)
    token = add([partial[2, 0], *got2, middle[1]], token, rows=part[1])
    pairs[1] = z_perm(token, PAIRS)

    terms = [after(partial[3, 0], *scales_x), *got3, last, tuple(pairs)]
    states = [master, first_moment, second_moment]
    factor = 1.0 / math.sqrt(acts.shape[0] * n_dp)
    (owned,) = update(terms, states, factor, [3], "weights")

    low, between = z < 2, (z == 1) | (z == 2)
    sources = [z, z ^ 1, jnp.where(low, 2, 1), jnp.where(low, 3, 0)]
    over0 = [x_perm(owned, by) for by in others]
    pairs, mid = z_perm(owned, PAIRS), z_perm(owned, MIDDLE)
    new_master, new_first, new_second = update(
        [after(terms[0], owned), *terms[1:]], states, factor, [0, 1, 2], "states"
    )
    scales = after(scales, owned)
    for got in scales_x:
        scales = jnp.maximum(scales, got)
    scales_z = z_perm(scales, PAIRS)

    come = [pairs, mid, new_master]
    mid_far, outwards = z_perm(after(pairs, *come), MIDDLE), z_perm(after(mid, *come), OUTWARDS)
    over1 = [x_perm(after(pairs, *come), by) for by in others]
    weights = blank((rows, columns), BF16)

    def put(weights, value, slot, by, h=0):
        at = (sources[slot] * n_x + (x - by) % n_x) * width
        return lax.dynamic_update_slice(weights, value, (h * half, at))

    weights = put(weights, owned, 0, 0)
    weights = put(weights, pairs, 1, 0)
    come = [mid_far, outwards, *over0]
    near = lax.optimization_barrier(jnp.where(between, after(mid, *come), outwards))
    far = [z_perm(after(lax.slice_in_dim(mid_far, h * half, (h + 1) * half), *come), OUTWARDS) for h in halves]
    over2 = [x_perm(near, by) for by in others]
    scales = after(scales, scales_z, near)
    scales = jnp.maximum(scales, scales_z)
    scales_z = z_perm(scales, [(a, a ^ 2) for a in range(Z)])
    for got, by in zip(over0, others):
        weights = put(weights, got, 0, by)
    weights = put(after(weights, near), near, 2, 0)
    for got, by in zip(over1, others):
        weights = put(weights, got, 1, by)
    distant, over3 = [None] * 2, [None] * 2
    for h in halves:
        come = [far[h], *over1] if h == 0 else [far[h], distant[0]]
        value = after(lax.slice_in_dim(mid_far, h * half, (h + 1) * half), *come)
        distant[h] = lax.optimization_barrier(jnp.where(between, value, far[h]))
        over3[h] = [x_perm(distant[h], by) for by in others]
    for h in halves:
        weights = put(weights, distant[h], 3, 0, h)
    for got, by in zip(over2, others):
        weights = put(weights, got, 2, by)
    for h in halves:
        for got, by in zip(over3[h], others):
            weights = put(weights, got, 3, by, h)
    block_scales = jnp.maximum(scales, after(scales_z, *distant)) + 1e-06
    return (new_master, new_first, new_second, weights, block_scales)


def solution(mesh):
    in_specs = (
        P("dp", "tensor"),
        P(("dp", "tensor"), None),
        P("tensor", "dp"),
        P("tensor", "dp"),
        P("tensor", "dp"),
    )
    out_specs = (
        P("tensor", "dp"),
        P("tensor", "dp"),
        P("tensor", "dp"),
        P("tensor", None),
        P("tensor", None),
    )
    return jax.shard_map(body, mesh=mesh, in_specs=in_specs, out_specs=out_specs, check_vma=False)
```

```python
import math

import jax
import jax.numpy as jnp
from jax import lax
from jax.experimental import pallas as pl
from jax.experimental.pallas import tpu as pltpu
from jax.sharding import PartitionSpec as P

BLOCK = 128
Z = 4
F32 = jnp.float32
BF16 = jnp.bfloat16
VMEM = pl.BlockSpec(memory_space=pltpu.VMEM)
FREE = pl.CostEstimate(flops=0, bytes_accessed=0, transcendentals=0)

INWARDS = ((0, 1), (3, 2))
OUTWARDS = ((1, 0), (2, 3))
MIDDLE = ((1, 2), (2, 1))
PAIRS = ((0, 1), (1, 0), (2, 3), (3, 2))


def owner_z(z, slot):
    low = z < 2
    if slot == 3:
        return z
    if slot == 0:
        return jnp.where(low, 3, 0)
    end = (z == 0) | (z == Z - 1)
    two, one = jnp.where(low, 2, 1), jnp.where(end, jnp.where(low, 1, 2), jnp.where(low, 0, 3))
    return two if slot == 1 else one


def call(kernel, out_shape, operands, name):
    return pl.pallas_call(
        kernel,
        out_shape=list(out_shape),
        in_specs=[VMEM] * len(operands),
        out_specs=[VMEM] * len(out_shape),
        cost_estimate=FREE,
        name=name,
    )


def arrange(cot, pieces, width, n_x):
    def kernel(cot_ref, *outs):
        owner = lax.axis_index("dp")
        z, x = owner // n_x, owner % n_x
        for piece, out in zip(pieces, outs):
            for j, (slot, by) in enumerate(piece):
                at = pl.multiple_of((owner_z(z, slot) * n_x + (x + by) % n_x) * width, width)
                out[:, j * width : (j + 1) * width] = cot_ref[:, pl.ds(at, width)]

    shapes = [jax.ShapeDtypeStruct((cot.shape[0], len(piece) * width), BF16) for piece in pieces]
    return call(kernel, shapes, [cot], "arrange")(cot)


def multiply(acts_t, group, chunks, width, cost):
    rows, tokens = acts_t.shape
    depth, columns = group[0].shape
    step = min(rows, 512)
    blocks = step // BLOCK

    def kernel(acts_ref, *refs):
        parts, outs, top, cot = refs[: len(group)], refs[len(group) : -2], refs[-2], refs[-1]

        @pl.when(pl.program_id(0) == 0)
        def _():
            seat = lax.axis_index("tensor")
            for k, part in enumerate(parts):
                cot[pl.ds(pl.multiple_of((seat ^ k) * depth, depth), depth), :] = part[...]

        for j in range(chunks):
            here = slice(j * width, (j + 1) * width)
            acc = jnp.dot(acts_ref[...], cot[:, here], preferred_element_type=F32)
            top[0, :, here] = jnp.max(jnp.abs(acc).reshape(blocks, BLOCK, width), axis=1)
            outs[j][...] = acc.astype(BF16)

    out = pl.pallas_call(
        kernel,
        grid=(rows // step,),
        in_specs=[pl.BlockSpec((step, tokens), lambda i: (i, 0))]
        + [pl.BlockSpec((depth, columns), lambda i: (0, 0))] * len(group),
        out_specs=[pl.BlockSpec((step, width), lambda i: (i, 0))] * chunks
        + [pl.BlockSpec((1, blocks, columns), lambda i: (i, 0, 0))],
        out_shape=[jax.ShapeDtypeStruct((rows, width), BF16)] * chunks
        + [jax.ShapeDtypeStruct((rows // step, blocks, columns), F32)],
        scratch_shapes=[pltpu.VMEM((tokens, columns), BF16)],
        compiler_params=pltpu.CompilerParams(vmem_limit_bytes=48 * 1024 * 1024),
        cost_estimate=cost,
        name="partials",
    )(acts_t, *group)
    return out[:chunks], out[chunks]


def add(terms, *earlier, rows=None):
    held = lax.optimization_barrier((*terms, *earlier))[: len(terms)]
    if rows is not None:
        held = [term if term.shape[0] == rows[1] else lax.slice_in_dim(term, rows[0], sum(rows)) for term in held]
    total = held[0].astype(F32)
    for term in held[1:]:
        total = total + term.astype(F32)
    return lax.optimization_barrier(total.astype(BF16))


def adamw(terms, states, factor):
    total = terms[0].astype(F32)
    for term in terms[1:]:
        total = total + term.astype(F32)
    master, first_moment, second_moment = states
    gradient = total * factor
    new_first = 0.9 * first_moment + 0.1 * gradient
    new_second = 0.95 * second_moment + 0.05 * gradient * gradient
    first_hat = new_first * (1.0 / (1.0 - 0.9**10))
    second_hat = new_second * (1.0 / (1.0 - 0.95**10))
    new_master = master * (1.0 - 0.01 * 0.1) - 0.01 * first_hat / (jnp.sqrt(second_hat) + 1e-08)
    return new_master, new_first, new_second, new_master.astype(BF16)


def update(terms, states, factor, wanted, name):
    rows, width = states[0].shape
    step = min(rows // 2, 512)
    half = rows // 2 // step
    flat = [value for term in terms for value in (term if isinstance(term, tuple) else (term,))]
    dtypes = [(F32, F32, F32, BF16)[k] for k in wanted]

    def kernel(*refs):
        ins, outs = refs[: len(flat) + 3], refs[len(flat) + 3 :]
        values, at = [], 0
        for term in terms:
            if isinstance(term, tuple):
                values.append(jnp.where(pl.program_id(0) < half, ins[at][...], ins[at + 1][...]))
                at += 2
            else:
                values.append(ins[at][...])
                at += 1
        results = adamw(values, [ref[...] for ref in ins[at:]], factor)
        for out, k in zip(outs, wanted):
            out[...] = results[k]

    whole = pl.BlockSpec((step, width), lambda i: (i, 0))
    halves = [
        pl.BlockSpec((step, width), lambda i: (jnp.minimum(i, half - 1), 0)),
        pl.BlockSpec((step, width), lambda i: (jnp.maximum(i - half, 0), 0)),
    ]
    specs = [spec for term in terms for spec in (halves if isinstance(term, tuple) else [whole])]
    return pl.pallas_call(
        kernel,
        grid=(rows // step,),
        in_specs=specs + [whole] * 3,
        out_specs=[whole] * len(wanted),
        out_shape=[jax.ShapeDtypeStruct((rows, width), dtype) for dtype in dtypes],
        compiler_params=pltpu.CompilerParams(vmem_limit_bytes=48 * 1024 * 1024),
        cost_estimate=FREE,
        name=name,
    )(*flat, *states)


def blank(shape, dtype):
    return pl.pallas_call(
        lambda ref: None,
        out_specs=pl.BlockSpec(memory_space=pl.ANY),
        out_shape=jax.ShapeDtypeStruct(shape, dtype),
        cost_estimate=FREE,
        name="blank",
    )()


def after(value, *earlier):
    return lax.optimization_barrier((value, *earlier))[0] if earlier else value


def body(acts, cotangent, master, first_moment, second_moment):
    n_dp = lax.axis_size("dp")
    n_tensor = lax.axis_size("tensor")
    n_x = n_dp // Z
    owner = lax.axis_index("dp")
    z, x = owner // n_x, owner % n_x
    rows, columns = acts.shape[1], cotangent.shape[1]
    width = columns // n_dp
    high = width // BLOCK
    others = range(1, n_x)

    def z_perm(value, pairs):
        return lax.ppermute(value, "dp", [(a * n_x + i, b * n_x + i) for a, b in pairs for i in range(n_x)])

    def x_perm(value, by, where=range(Z)):
        pairs = [(a * n_x + i, a * n_x + (i + by) % n_x) for a in where for i in range(n_x)]
        return lax.ppermute(value, "dp", pairs)

    def seat_perm(value, flip):
        return lax.ppermute(value, "tensor", [(i, i ^ flip) for i in range(n_tensor)])

    pieces = [
        [(0, by) for by in others],
        [(0, 0)] + [(1, by) for by in others],
        [(i, by) for i in (2, 3) for by in others] + [(1, 0), (2, 0), (3, 0)],
    ]
    own = arrange(cotangent, pieces, width, n_x)
    partial, tops, across = {}, [], []

    def fetch(piece, *earlier):
        value = after(own[piece], *earlier)
        across.append([value] + [seat_perm(value, k) for k in range(2, n_tensor, 2)])

    def partials(piece, *earlier):
        group = [part for value in across[piece] for part in (value, seat_perm(after(value, *earlier), 1))]
        cost = FREE if piece else pl.CostEstimate(flops=10**10, bytes_accessed=acts.size, transcendentals=0)
        chunks, top = multiply(after(acts_t, *earlier), group, len(pieces[piece]), width, cost)
        partial.update(zip(pieces[piece], chunks))
        tops.append(top)
        return chunks[0]

    def send_x(slot):
        return [x_perm(partial[slot, by], by) for by in others]

    half = rows // 2
    halves = range(2)
    part = [(h * half, half) for h in halves]

    for piece in range(len(pieces)):
        fetch(piece)
    acts_t = after(acts, *own).T
    token = partials(0, acts_t)
    got0 = send_x(0)
    token = partials(1, token)
    got1 = send_x(1)
    far, middle = [None] * 2, [None] * 2
    for h in halves:
        token = add([partial[0, 0], *got0], token, rows=part[h])
        far[h] = z_perm(token, INWARDS)
    token = partials(2, token)
    got2, got3 = send_x(2), send_x(3)
    token = add([partial[1, 0], *got1], token)
    inwards = z_perm(token, INWARDS)
    for h in halves:
        token = add([partial[0, 0], *got0, far[h]], token, rows=part[h])
        middle[h] = z_perm(token, MIDDLE)

    top = jnp.concatenate([after(t, token).reshape(rows // BLOCK, -1, BLOCK).max(axis=2) for t in tops], axis=1)
    column = jnp.stack(
        [(owner_z(z, i) * n_x + (x + by) % n_x) * high + h for piece in pieces for i, by in piece for h in range(high)]
    )
    here = column[None, :, None] == jnp.arange(n_dp * high)[None, None, :]
    scales = jnp.max(jnp.where(here, top[:, :, None], 0.0), axis=1)
    scales_x = [x_perm(scales, by) for by in others]

    pairs = [None] * 2
    token = add([partial[2, 0], *got2, middle[0]], scales, rows=part[0])
    pairs[0] = z_perm(token, PAIRS)
    token = add([partial[1, 0], *got1, inwards], token)
    last = z_perm(token, MIDDLE)
    token = add([partial[2, 0], *got2, middle[1]], token, pairs[0], rows=part[1])
    pairs[1] = z_perm(token, PAIRS)

    terms = [after(partial[3, 0], *scales_x), *got3, last, tuple(pairs)]
    states = [master, first_moment, second_moment]
    factor = 1.0 / math.sqrt(acts.shape[0] * n_dp)
    (owned,) = update(terms, states, factor, [3], "weights")

    low, between = z < 2, (z == 1) | (z == 2)
    sources = [z, z ^ 1, jnp.where(low, 2, 1), jnp.where(low, 3, 0)]
    over0 = [x_perm(owned, by) for by in others]
    pairs, mid = z_perm(owned, PAIRS), z_perm(owned, MIDDLE)
    new_master, new_first, new_second = update(
        [after(terms[0], owned), *terms[1:]], states, factor, [0, 1, 2], "states"
    )
    come = [pairs, mid, new_master, *over0]
    over1 = [x_perm(after(pairs, *come), by) for by in others]
    mid_far, outwards = z_perm(after(pairs, *come), MIDDLE), z_perm(after(mid, *come), OUTWARDS)
    come = [mid_far, outwards]
    near = lax.optimization_barrier(jnp.where(between, after(mid, *come, *over1), outwards))
    over2 = [x_perm(near, by) for by in others]
    cuts = [lax.slice_in_dim(mid_far, h * half, (h + 1) * half) for h in halves]
    far = [z_perm(after(cuts[0], *come), OUTWARDS), z_perm(after(cuts[1], near), OUTWARDS)]

    def put(weights, value, slot, by, h=0):
        at = (sources[slot] * n_x + (x - by) % n_x) * width
        return lax.dynamic_update_slice(weights, value, (h * half, at))

    weights = after(blank((rows, columns), BF16), near)
    weights = put(weights, owned, 0, 0)
    weights = put(weights, pairs, 1, 0)
    weights = put(weights, near, 2, 0)
    for over, slot in ((over0, 0), (over1, 1)):
        for got, by in zip(over, others):
            weights = put(weights, got, slot, by)
    distant, over3 = [None] * 2, [None] * 2
    for h in halves:
        value = after(lax.slice_in_dim(mid_far, h * half, (h + 1) * half), far[h], *distant[:h])
        distant[h] = lax.optimization_barrier(jnp.where(between, value, far[h]))
        over3[h] = [x_perm(distant[h], by) for by in others]
    for h in halves:
        weights = put(weights, distant[h], 3, 0, h)
    for got, by in zip(over2, others):
        weights = put(weights, got, 2, by)
    for h in halves:
        for got, by in zip(over3[h], others):
            weights = put(weights, got, 3, by, h)
    scales = after(scales, *distant, *over2)
    for got in scales_x:
        scales = jnp.maximum(scales, got)
    scales = jnp.maximum(scales, z_perm(scales, PAIRS))
    scales_z = z_perm(scales, [(a, a ^ 2) for a in range(Z)])
    block_scales = jnp.maximum(scales, scales_z) + 1e-06
    return (new_master, new_first, new_second, weights, block_scales)


def solution(mesh):
    in_specs = (
        P("dp", "tensor"),
        P(("dp", "tensor"), None),
        P("tensor", "dp"),
        P("tensor", "dp"),
        P("tensor", "dp"),
    )
    out_specs = (
        P("tensor", "dp"),
        P("tensor", "dp"),
        P("tensor", "dp"),
        P("tensor", None),
        P("tensor", None),
    )
    return jax.shard_map(body, mesh=mesh, in_specs=in_specs, out_specs=out_specs, check_vma=False)
```

```python
import math

import jax
import jax.numpy as jnp
from jax import lax
from jax.experimental import pallas as pl
from jax.experimental.pallas import tpu as pltpu
from jax.sharding import PartitionSpec as P

BLOCK = 128
Z = 4
F32 = jnp.float32
BF16 = jnp.bfloat16
VMEM = pl.BlockSpec(memory_space=pltpu.VMEM)
FREE = pl.CostEstimate(flops=0, bytes_accessed=0, transcendentals=0)

INWARDS = ((0, 1), (3, 2))
OUTWARDS = ((1, 0), (2, 3))
MIDDLE = ((1, 2), (2, 1))
PAIRS = ((0, 1), (1, 0), (2, 3), (3, 2))


def owner_z(z, slot):
    low = z < 2
    if slot == 3:
        return z
    if slot == 0:
        return jnp.where(low, 3, 0)
    end = (z == 0) | (z == Z - 1)
    two, one = jnp.where(low, 2, 1), jnp.where(end, jnp.where(low, 1, 2), jnp.where(low, 0, 3))
    return two if slot == 1 else one


def call(kernel, out_shape, operands, name):
    return pl.pallas_call(
        kernel,
        out_shape=list(out_shape),
        in_specs=[VMEM] * len(operands),
        out_specs=[VMEM] * len(out_shape),
        cost_estimate=FREE,
        name=name,
    )


def arrange(cot, pieces, width, n_x):
    def kernel(cot_ref, *outs):
        owner = lax.axis_index("dp")
        z, x = owner // n_x, owner % n_x
        for piece, out in zip(pieces, outs):
            for j, (slot, by) in enumerate(piece):
                at = pl.multiple_of((owner_z(z, slot) * n_x + (x + by) % n_x) * width, width)
                out[:, j * width : (j + 1) * width] = cot_ref[:, pl.ds(at, width)]

    shapes = [jax.ShapeDtypeStruct((cot.shape[0], len(piece) * width), BF16) for piece in pieces]
    return call(kernel, shapes, [cot], "arrange")(cot)


def multiply(acts_t, group, first, chunks, width):
    rows, tokens = acts_t.shape
    depth = group[0].shape[0]
    columns, left = chunks * width, first * width
    step = min(rows, 512)
    blocks = step // BLOCK

    def kernel(acts_ref, *refs):
        parts, outs, top, cot = refs[: len(group)], refs[len(group) : -2], refs[-2], refs[-1]

        @pl.when(pl.program_id(0) == 0)
        def _():
            seat = lax.axis_index("tensor")
            for k, part in enumerate(parts):
                at = pl.multiple_of((seat ^ k) * depth, depth)
                cot[pl.ds(at, depth), :] = part[:, left : left + columns]

        for j in range(chunks):
            here = slice(j * width, (j + 1) * width)
            acc = jnp.dot(acts_ref[...], cot[:, here], preferred_element_type=F32)
            top[0, :, here] = jnp.max(jnp.abs(acc).reshape(blocks, BLOCK, width), axis=1)
            outs[j][...] = acc.astype(BF16)

    out = pl.pallas_call(
        kernel,
        grid=(rows // step,),
        in_specs=[pl.BlockSpec((step, tokens), lambda i: (i, 0))]
        + [pl.BlockSpec(group[0].shape, lambda i: (0, 0))] * len(group),
        out_specs=[pl.BlockSpec((step, width), lambda i: (i, 0))] * chunks
        + [pl.BlockSpec((1, blocks, columns), lambda i: (i, 0, 0))],
        out_shape=[jax.ShapeDtypeStruct((rows, width), BF16)] * chunks
        + [jax.ShapeDtypeStruct((rows // step, blocks, columns), F32)],
        scratch_shapes=[pltpu.VMEM((tokens, columns), BF16)],
        compiler_params=pltpu.CompilerParams(vmem_limit_bytes=48 * 1024 * 1024),
        cost_estimate=FREE,
        name="partials",
    )(acts_t, *group)
    return out[:chunks], out[chunks]


def add(terms, *earlier, rows=None):
    held = lax.optimization_barrier((*terms, *earlier))[: len(terms)]
    if rows is not None:
        held = [term if term.shape[0] == rows[1] else lax.slice_in_dim(term, rows[0], sum(rows)) for term in held]
    total = held[0].astype(F32)
    for term in held[1:]:
        total = total + term.astype(F32)
    return lax.optimization_barrier(total.astype(BF16))


def adamw(terms, states, factor):
    total = terms[0].astype(F32)
    for term in terms[1:]:
        total = total + term.astype(F32)
    master, first_moment, second_moment = states
    gradient = total * factor
    new_first = 0.9 * first_moment + 0.1 * gradient
    new_second = 0.95 * second_moment + 0.05 * gradient * gradient
    first_hat = new_first * (1.0 / (1.0 - 0.9**10))
    second_hat = new_second * (1.0 / (1.0 - 0.95**10))
    new_master = master * (1.0 - 0.01 * 0.1) - 0.01 * first_hat / (jnp.sqrt(second_hat) + 1e-08)
    return new_master, new_first, new_second, new_master.astype(BF16)


def update(terms, states, factor, wanted, name):
    rows, width = states[0].shape
    step = min(rows // 2, 512)
    half = rows // 2 // step
    flat = [value for term in terms for value in (term if isinstance(term, tuple) else (term,))]
    dtypes = [(F32, F32, F32, BF16)[k] for k in wanted]

    def kernel(*refs):
        ins, outs = refs[: len(flat) + 3], refs[len(flat) + 3 :]
        values, at = [], 0
        for term in terms:
            if isinstance(term, tuple):
                values.append(jnp.where(pl.program_id(0) < half, ins[at][...], ins[at + 1][...]))
                at += 2
            else:
                values.append(ins[at][...])
                at += 1
        results = adamw(values, [ref[...] for ref in ins[at:]], factor)
        for out, k in zip(outs, wanted):
            out[...] = results[k]

    whole = pl.BlockSpec((step, width), lambda i: (i, 0))
    halves = [
        pl.BlockSpec((step, width), lambda i: (jnp.minimum(i, half - 1), 0)),
        pl.BlockSpec((step, width), lambda i: (jnp.maximum(i - half, 0), 0)),
    ]
    specs = [spec for term in terms for spec in (halves if isinstance(term, tuple) else [whole])]
    return pl.pallas_call(
        kernel,
        grid=(rows // step,),
        in_specs=specs + [whole] * 3,
        out_specs=[whole] * len(wanted),
        out_shape=[jax.ShapeDtypeStruct((rows, width), dtype) for dtype in dtypes],
        compiler_params=pltpu.CompilerParams(vmem_limit_bytes=48 * 1024 * 1024),
        cost_estimate=FREE,
        name=name,
    )(*flat, *states)


def blank(shape, dtype):
    return pl.pallas_call(
        lambda ref: None,
        out_specs=pl.BlockSpec(memory_space=pl.ANY),
        out_shape=jax.ShapeDtypeStruct(shape, dtype),
        cost_estimate=FREE,
        name="blank",
    )()


def after(value, *earlier):
    return lax.optimization_barrier((value, *earlier))[0] if earlier else value


def tie(*values):
    return lax.optimization_barrier(values)


def body(acts, cotangent, master, first_moment, second_moment):
    n_dp = lax.axis_size("dp")
    n_tensor = lax.axis_size("tensor")
    n_x = n_dp // Z
    owner = lax.axis_index("dp")
    z, x = owner // n_x, owner % n_x
    rows, columns = acts.shape[1], cotangent.shape[1]
    width = columns // n_dp
    high = width // BLOCK
    others = range(1, n_x)

    def z_perm(value, pairs):
        return lax.ppermute(value, "dp", [(a * n_x + i, b * n_x + i) for a, b in pairs for i in range(n_x)])

    def x_perm(value, by, where=range(Z)):
        pairs = [(a * n_x + i, a * n_x + (i + by) % n_x) for a in where for i in range(n_x)]
        return lax.ppermute(value, "dp", pairs)

    def seat_perm(value, flip):
        return lax.ppermute(value, "tensor", [(i, i ^ flip) for i in range(n_tensor)])

    pieces = [
        [(0, by) for by in others] + [(0, 0)] + [(1, by) for by in others],
        [(i, by) for i in (2, 3) for by in others] + [(1, 0), (2, 0), (3, 0)],
    ]
    own = arrange(cotangent, pieces, width, n_x)
    partial, tops, across = {}, [], []

    def fetch(piece, *earlier):
        value = after(own[piece], *earlier)
        across.append([value] + [seat_perm(value, k) for k in range(2, n_tensor, 2)])

    def both_cores(piece, *earlier):
        return [part for value in across[piece] for part in (value, seat_perm(after(value, *earlier), 1))]

    def partials(group, which, first, *earlier):
        chunks, top = multiply(after(acts_t, *earlier), group, first, len(which), width)
        partial.update(zip(which, chunks))
        tops.append(top)
        return chunks[0]

    def send_x(slot):
        return [x_perm(partial[slot, by], by) for by in others]

    half = rows // 2
    halves = range(2)
    part = [(h * half, half) for h in halves]

    for piece in range(len(pieces)):
        fetch(piece)
    acts_t = after(acts, *own).T
    group = both_cores(0, acts_t)
    sent = len(others)
    token = partials(group, pieces[0][:sent], 0, acts_t)
    got0 = send_x(0)
    token = partials(group, pieces[0][sent:], sent, token)
    got1 = send_x(1)
    far, middle = [None] * 2, [None] * 2
    for h in halves:
        token = add([partial[0, 0], *got0], token, rows=part[h])
        far[h] = z_perm(token, INWARDS)
    token = partials(both_cores(1, token), pieces[1], 0, token)
    got2, got3 = send_x(2), send_x(3)
    token = add([partial[1, 0], *got1], token)
    inwards = z_perm(token, INWARDS)
    for h in halves:
        token = add([partial[0, 0], *got0, far[h]], token, rows=part[h])
        middle[h] = z_perm(token, MIDDLE)

    top = jnp.concatenate([after(t, token).reshape(rows // BLOCK, -1, BLOCK).max(axis=2) for t in tops], axis=1)
    column = jnp.stack(
        [(owner_z(z, i) * n_x + (x + by) % n_x) * high + h for piece in pieces for i, by in piece for h in range(high)]
    )
    here = column[None, :, None] == jnp.arange(n_dp * high)[None, None, :]
    scales = jnp.max(jnp.where(here, top[:, :, None], 0.0), axis=1)
    scales_x = [x_perm(scales, by) for by in others]

    pairs = [None] * 2
    token = add([partial[2, 0], *got2, middle[0]], scales, rows=part[0])
    pairs[0] = z_perm(token, PAIRS)
    token = add([partial[1, 0], *got1, inwards], token)
    last = z_perm(token, MIDDLE)
    token = add([partial[2, 0], *got2, middle[1]], token, pairs[0], rows=part[1])
    pairs[1] = z_perm(token, PAIRS)

    terms = [after(partial[3, 0], *scales_x), *got3, last, tuple(pairs)]
    states = [master, first_moment, second_moment]
    factor = 1.0 / math.sqrt(acts.shape[0] * n_dp)
    (owned,) = update(terms, states, factor, [3], "weights")

    low, between = z < 2, (z == 1) | (z == 2)
    sources = [z, z ^ 1, jnp.where(low, 2, 1), jnp.where(low, 3, 0)]
    terms[0], owned = tie(terms[0], owned)
    new_master, new_first, new_second = update(terms, states, factor, [0, 1, 2], "states")
    over0 = [x_perm(owned, by) for by in others]
    pairs, mid = z_perm(owned, PAIRS), z_perm(owned, MIDDLE)
    def put(weights, value, slot, by, h=0):
        at = (sources[slot] * n_x + (x - by) % n_x) * width
        return lax.dynamic_update_slice(weights, value, (h * half, at))

    weights = blank((rows, columns), BF16)
    for got, by in zip(over0, others):
        weights = put(weights, got, 0, by)
    weights = put(weights, pairs, 1, 0)
    pairs, mid, weights = tie(pairs, mid, weights)
    over1 = [x_perm(pairs, by) for by in others]
    mid_far, outwards = z_perm(pairs, MIDDLE), z_perm(mid, OUTWARDS)
    for got, by in zip(over1, others):
        weights = put(weights, got, 1, by)
    mid, mid_far, outwards, weights = tie(mid, mid_far, outwards, weights)
    (near,) = tie(jnp.where(between, mid, outwards))
    over2 = [x_perm(near, by) for by in others]
    cuts = [lax.slice_in_dim(mid_far, h * half, (h + 1) * half) for h in halves]
    far = [z_perm(cuts[0], OUTWARDS), None]
    cuts[1], near = tie(cuts[1], near)
    far[1] = z_perm(cuts[1], OUTWARDS)
    weights, near = tie(weights, near)
    weights = put(weights, owned, 0, 0)
    weights = put(weights, near, 2, 0)
    distant, over3 = [None] * 2, [None] * 2
    for h in halves:
        (distant[h],) = tie(jnp.where(between, cuts[h], far[h]))
        over3[h] = [x_perm(distant[h], by) for by in others]
        if h == 0:
            far[1], distant[0] = tie(far[1], distant[0])
    for h in halves:
        weights = put(weights, distant[h], 3, 0, h)
    for got, by in zip(over2, others):
        weights = put(weights, got, 2, by)
    for h in halves:
        for got, by in zip(over3[h], others):
            weights = put(weights, got, 3, by, h)
    scales = after(scales, *distant, *over2)
    for got in scales_x:
        scales = jnp.maximum(scales, got)
    scales = jnp.maximum(scales, z_perm(scales, PAIRS))
    scales_z = z_perm(scales, [(a, a ^ 2) for a in range(Z)])
    block_scales = jnp.maximum(scales, scales_z) + 1e-06
    return (new_master, new_first, new_second, weights, block_scales)


def solution(mesh):
    in_specs = (
        P("dp", "tensor"),
        P(("dp", "tensor"), None),
        P("tensor", "dp"),
        P("tensor", "dp"),
        P("tensor", "dp"),
    )
    out_specs = (
        P("tensor", "dp"),
        P("tensor", "dp"),
        P("tensor", "dp"),
        P("tensor", None),
        P("tensor", None),
    )
    return jax.shard_map(body, mesh=mesh, in_specs=in_specs, out_specs=out_specs, check_vma=False)
```

```python
import math

import jax
import jax.numpy as jnp
from jax import lax
from jax.experimental import pallas as pl
from jax.experimental.pallas import tpu as pltpu
from jax.sharding import PartitionSpec as P

BLOCK = 128
Z = 4
F32 = jnp.float32
BF16 = jnp.bfloat16
VMEM = pl.BlockSpec(memory_space=pltpu.VMEM)
FREE = pl.CostEstimate(flops=0, bytes_accessed=0, transcendentals=0)

INWARDS = ((0, 1), (3, 2))
OUTWARDS = ((1, 0), (2, 3))
MIDDLE = ((1, 2), (2, 1))
PAIRS = ((0, 1), (1, 0), (2, 3), (3, 2))


def owner_z(z, slot):
    low = z < 2
    if slot == 3:
        return z
    if slot == 0:
        return jnp.where(low, 3, 0)
    end = (z == 0) | (z == Z - 1)
    two, one = jnp.where(low, 2, 1), jnp.where(end, jnp.where(low, 1, 2), jnp.where(low, 0, 3))
    return two if slot == 1 else one


def call(kernel, out_shape, operands, name):
    return pl.pallas_call(
        kernel,
        out_shape=list(out_shape),
        in_specs=[VMEM] * len(operands),
        out_specs=[VMEM] * len(out_shape),
        cost_estimate=FREE,
        name=name,
    )


def arrange(cot, pieces, width, n_x):
    def kernel(cot_ref, *outs):
        owner = lax.axis_index("dp")
        z, x = owner // n_x, owner % n_x
        for piece, out in zip(pieces, outs):
            for j, (slot, by) in enumerate(piece):
                at = pl.multiple_of((owner_z(z, slot) * n_x + (x + by) % n_x) * width, width)
                out[:, j * width : (j + 1) * width] = cot_ref[:, pl.ds(at, width)]

    shapes = [jax.ShapeDtypeStruct((cot.shape[0], len(piece) * width), BF16) for piece in pieces]
    return call(kernel, shapes, [cot], "arrange")(cot)


def multiply(acts_t, group, chunks, width, cost):
    rows, tokens = acts_t.shape
    depth, columns = group[0].shape
    step = min(rows, 512)
    blocks = step // BLOCK

    def kernel(acts_ref, *refs):
        parts, outs, top, cot = refs[: len(group)], refs[len(group) : -2], refs[-2], refs[-1]

        @pl.when(pl.program_id(0) == 0)
        def _():
            seat = lax.axis_index("tensor")
            for k, part in enumerate(parts):
                cot[pl.ds(pl.multiple_of((seat ^ k) * depth, depth), depth), :] = part[...]

        for j in range(chunks):
            here = slice(j * width, (j + 1) * width)
            acc = jnp.dot(acts_ref[...], cot[:, here], preferred_element_type=F32)
            top[0, :, here] = jnp.max(jnp.abs(acc).reshape(blocks, BLOCK, width), axis=1)
            outs[j][...] = acc.astype(BF16)

    out = pl.pallas_call(
        kernel,
        grid=(rows // step,),
        in_specs=[pl.BlockSpec((step, tokens), lambda i: (i, 0))]
        + [pl.BlockSpec((depth, columns), lambda i: (0, 0))] * len(group),
        out_specs=[pl.BlockSpec((step, width), lambda i: (i, 0))] * chunks
        + [pl.BlockSpec((1, blocks, columns), lambda i: (i, 0, 0))],
        out_shape=[jax.ShapeDtypeStruct((rows, width), BF16)] * chunks
        + [jax.ShapeDtypeStruct((rows // step, blocks, columns), F32)],
        scratch_shapes=[pltpu.VMEM((tokens, columns), BF16)],
        compiler_params=pltpu.CompilerParams(vmem_limit_bytes=48 * 1024 * 1024),
        cost_estimate=cost,
        name="partials",
    )(acts_t, *group)
    return out[:chunks], out[chunks]


def add(terms, *earlier, rows=None):
    held = lax.optimization_barrier((*terms, *earlier))[: len(terms)]
    if rows is not None:
        held = [term if term.shape[0] == rows[1] else lax.slice_in_dim(term, rows[0], sum(rows)) for term in held]
    total = held[0].astype(F32)
    for term in held[1:]:
        total = total + term.astype(F32)
    return lax.optimization_barrier(total.astype(BF16))


def adamw(terms, states, factor):
    total = terms[0].astype(F32)
    for term in terms[1:]:
        total = total + term.astype(F32)
    master, first_moment, second_moment = states
    gradient = total * factor
    new_first = 0.9 * first_moment + 0.1 * gradient
    new_second = 0.95 * second_moment + 0.05 * gradient * gradient
    first_hat = new_first * (1.0 / (1.0 - 0.9**10))
    second_hat = new_second * (1.0 / (1.0 - 0.95**10))
    new_master = master * (1.0 - 0.01 * 0.1) - 0.01 * first_hat / (jnp.sqrt(second_hat) + 1e-08)
    return new_master, new_first, new_second, new_master.astype(BF16)


def update(terms, states, factor, wanted, name):
    rows, width = states[0].shape
    step = min(rows // 2, 512)
    half = rows // 2 // step
    flat = [value for term in terms for value in (term if isinstance(term, tuple) else (term,))]
    dtypes = [(F32, F32, F32, BF16)[k] for k in wanted]

    def kernel(*refs):
        ins, outs = refs[: len(flat) + 3], refs[len(flat) + 3 :]
        values, at = [], 0
        for term in terms:
            if isinstance(term, tuple):
                values.append(jnp.where(pl.program_id(0) < half, ins[at][...], ins[at + 1][...]))
                at += 2
            else:
                values.append(ins[at][...])
                at += 1
        results = adamw(values, [ref[...] for ref in ins[at:]], factor)
        for out, k in zip(outs, wanted):
            out[...] = results[k]

    whole = pl.BlockSpec((step, width), lambda i: (i, 0))
    halves = [
        pl.BlockSpec((step, width), lambda i: (jnp.minimum(i, half - 1), 0)),
        pl.BlockSpec((step, width), lambda i: (jnp.maximum(i - half, 0), 0)),
    ]
    specs = [spec for term in terms for spec in (halves if isinstance(term, tuple) else [whole])]
    return pl.pallas_call(
        kernel,
        grid=(rows // step,),
        in_specs=specs + [whole] * 3,
        out_specs=[whole] * len(wanted),
        out_shape=[jax.ShapeDtypeStruct((rows, width), dtype) for dtype in dtypes],
        compiler_params=pltpu.CompilerParams(vmem_limit_bytes=48 * 1024 * 1024),
        cost_estimate=FREE,
        name=name,
    )(*flat, *states)


def blank(shape, dtype):
    return pl.pallas_call(
        lambda ref: None,
        out_specs=pl.BlockSpec(memory_space=pl.ANY),
        out_shape=jax.ShapeDtypeStruct(shape, dtype),
        cost_estimate=FREE,
        name="blank",
    )()


def after(value, *earlier):
    return lax.optimization_barrier((value, *earlier))[0] if earlier else value


def body(acts, cotangent, master, first_moment, second_moment):
    n_dp = lax.axis_size("dp")
    n_tensor = lax.axis_size("tensor")
    n_x = n_dp // Z
    owner = lax.axis_index("dp")
    z, x = owner // n_x, owner % n_x
    rows, columns = acts.shape[1], cotangent.shape[1]
    width = columns // n_dp
    high = width // BLOCK
    others = range(1, n_x)

    def z_perm(value, pairs):
        return lax.ppermute(value, "dp", [(a * n_x + i, b * n_x + i) for a, b in pairs for i in range(n_x)])

    def x_perm(value, by, where=range(Z)):
        pairs = [(a * n_x + i, a * n_x + (i + by) % n_x) for a in where for i in range(n_x)]
        return lax.ppermute(value, "dp", pairs)

    def seat_perm(value, flip):
        return lax.ppermute(value, "tensor", [(i, i ^ flip) for i in range(n_tensor)])

    pieces = [
        [(0, by) for by in others],
        [(0, 0)] + [(1, by) for by in others],
        [(i, by) for i in (2, 3) for by in others] + [(1, 0), (2, 0), (3, 0)],
    ]
    own = arrange(cotangent, pieces, width, n_x)
    partial, tops, across = {}, [], []

    def fetch(piece, *earlier):
        value = after(own[piece], *earlier)
        across.append([value] + [seat_perm(value, k) for k in range(2, n_tensor, 2)])

    def partials(piece, *earlier):
        group = [part for value in across[piece] for part in (value, seat_perm(after(value, *earlier), 1))]
        cost = FREE if piece else pl.CostEstimate(flops=10**10, bytes_accessed=acts.size, transcendentals=0)
        chunks, top = multiply(after(acts_t, *earlier), group, len(pieces[piece]), width, cost)
        partial.update(zip(pieces[piece], chunks))
        tops.append(top)
        return chunks[0]

    def send_x(slot):
        return [x_perm(partial[slot, by], by) for by in others]

    half = rows // 2
    halves = range(2)
    part = [(h * half, half) for h in halves]

    for piece in range(len(pieces)):
        fetch(piece)
    acts_t = after(acts, *own).T
    token = partials(0, acts_t)
    got0 = send_x(0)
    token = partials(1, token)
    got1 = send_x(1)
    far, middle = [None] * 2, [None] * 2
    for h in halves:
        token = add([partial[0, 0], *got0], token, rows=part[h])
        far[h] = z_perm(token, INWARDS)
    token = partials(2, token)
    got2, got3 = send_x(2), send_x(3)
    token = add([partial[1, 0], *got1], token)
    inwards = z_perm(token, INWARDS)
    for h in halves:
        token = add([partial[0, 0], *got0, far[h]], token, rows=part[h])
        middle[h] = z_perm(token, MIDDLE)

    top = jnp.concatenate([after(t, token).reshape(rows // BLOCK, -1, BLOCK).max(axis=2) for t in tops], axis=1)
    column = jnp.stack(
        [(owner_z(z, i) * n_x + (x + by) % n_x) * high + h for piece in pieces for i, by in piece for h in range(high)]
    )
    here = column[None, :, None] == jnp.arange(n_dp * high)[None, None, :]
    scales = jnp.max(jnp.where(here, top[:, :, None], 0.0), axis=1)
    scales_x = [x_perm(scales, by) for by in others]

    pairs = [None] * 2
    token = add([partial[2, 0], *got2, middle[0]], scales, rows=part[0])
    pairs[0] = z_perm(token, PAIRS)
    token = add([partial[1, 0], *got1, inwards], token)
    last = z_perm(token, MIDDLE)
    token = add([partial[2, 0], *got2, middle[1]], token, pairs[0], rows=part[1])
    pairs[1] = z_perm(token, PAIRS)

    terms = [after(partial[3, 0], *scales_x), *got3, last, tuple(pairs)]
    states = [master, first_moment, second_moment]
    factor = 1.0 / math.sqrt(acts.shape[0] * n_dp)
    (owned,) = update(terms, states, factor, [3], "weights")

    low, between = z < 2, (z == 1) | (z == 2)
    sources = [z, z ^ 1, jnp.where(low, 2, 1), jnp.where(low, 3, 0)]
    over0 = [x_perm(owned, by) for by in others]
    pairs = z_perm(owned, PAIRS)
    mid = z_perm(owned, MIDDLE)
    new_master, new_first, new_second = update(
        [after(terms[0], owned), *terms[1:]], states, factor, [0, 1, 2], "states"
    )
    def put(weights, value, slot, by, h=0):
        at = (sources[slot] * n_x + (x - by) % n_x) * width
        return lax.dynamic_update_slice(weights, value, (h * half, at))

    weights = put(after(blank((rows, columns), BF16), new_master), owned, 0, 0)
    come = [pairs, mid, new_master, *over0]
    over1 = [x_perm(after(pairs, *come), by) for by in others]
    mid_far = z_perm(after(pairs, *come), MIDDLE)
    outwards = z_perm(after(mid, *come), OUTWARDS)
    weights = after(weights, mid_far)
    for got, by in zip(over0, others):
        weights = put(weights, got, 0, by)
    weights = put(weights, pairs, 1, 0)
    come = [mid_far, outwards]
    near = lax.optimization_barrier(jnp.where(between, after(mid, *come, *over1), outwards))
    over2 = [x_perm(near, by) for by in others]
    cuts = [lax.slice_in_dim(mid_far, h * half, (h + 1) * half) for h in halves]
    far = [z_perm(after(cuts[0], *come), OUTWARDS), z_perm(after(cuts[1], near), OUTWARDS)]
    weights = put(after(weights, near), near, 2, 0)
    for got, by in zip(over1, others):
        weights = put(weights, got, 1, by)
    distant, over3 = [None] * 2, [None] * 2
    for h in halves:
        value = after(lax.slice_in_dim(mid_far, h * half, (h + 1) * half), far[h], *distant[:h])
        distant[h] = lax.optimization_barrier(jnp.where(between, value, far[h]))
        over3[h] = [x_perm(distant[h], by) for by in others]
    for h in halves:
        weights = put(weights, distant[h], 3, 0, h)
    for got, by in zip(over2, others):
        weights = put(weights, got, 2, by)
    for h in halves:
        for got, by in zip(over3[h], others):
            weights = put(weights, got, 3, by, h)
    scales = after(scales, *distant, *over2)
    for got in scales_x:
        scales = jnp.maximum(scales, got)
    scales = jnp.maximum(scales, z_perm(scales, PAIRS))
    scales_z = z_perm(scales, [(a, a ^ 2) for a in range(Z)])
    block_scales = jnp.maximum(scales, scales_z) + 1e-06
    return (new_master, new_first, new_second, weights, block_scales)


def solution(mesh):
    in_specs = (
        P("dp", "tensor"),
        P(("dp", "tensor"), None),
        P("tensor", "dp"),
        P("tensor", "dp"),
        P("tensor", "dp"),
    )
    out_specs = (
        P("tensor", "dp"),
        P("tensor", "dp"),
        P("tensor", "dp"),
        P("tensor", None),
        P("tensor", None),
    )
    return jax.shard_map(body, mesh=mesh, in_specs=in_specs, out_specs=out_specs, check_vma=False)
```

```python
import math

import jax
import jax.numpy as jnp
from jax import lax
from jax.experimental import pallas as pl
from jax.experimental.pallas import tpu as pltpu
from jax.sharding import PartitionSpec as P

BLOCK = 128
Z = 4
F32 = jnp.float32
BF16 = jnp.bfloat16
VMEM = pl.BlockSpec(memory_space=pltpu.VMEM)
FREE = pl.CostEstimate(flops=0, bytes_accessed=0, transcendentals=0)

INWARDS = ((0, 1), (3, 2))
OUTWARDS = ((1, 0), (2, 3))
MIDDLE = ((1, 2), (2, 1))
PAIRS = ((0, 1), (1, 0), (2, 3), (3, 2))


def owner_z(z, slot):
    low = z < 2
    if slot == 3:
        return z
    if slot == 0:
        return jnp.where(low, 3, 0)
    end = (z == 0) | (z == Z - 1)
    two, one = jnp.where(low, 2, 1), jnp.where(end, jnp.where(low, 1, 2), jnp.where(low, 0, 3))
    return two if slot == 1 else one


def call(kernel, out_shape, operands, name):
    return pl.pallas_call(
        kernel,
        out_shape=list(out_shape),
        in_specs=[VMEM] * len(operands),
        out_specs=[VMEM] * len(out_shape),
        cost_estimate=FREE,
        name=name,
    )


def arrange(cot, pieces, width, n_x):
    def kernel(cot_ref, *outs):
        owner = lax.axis_index("dp")
        z, x = owner // n_x, owner % n_x
        for piece, out in zip(pieces, outs):
            for j, (slot, by) in enumerate(piece):
                at = pl.multiple_of((owner_z(z, slot) * n_x + (x + by) % n_x) * width, width)
                out[:, j * width : (j + 1) * width] = cot_ref[:, pl.ds(at, width)]

    shapes = [jax.ShapeDtypeStruct((cot.shape[0], len(piece) * width), BF16) for piece in pieces]
    return call(kernel, shapes, [cot], "arrange")(cot)


def multiply(acts_t, group, chunks, width, cost):
    rows, tokens = acts_t.shape
    depth, columns = group[0].shape
    step = min(rows, 512)
    blocks = step // BLOCK

    def kernel(acts_ref, *refs):
        parts, outs, top, cot = refs[: len(group)], refs[len(group) : -2], refs[-2], refs[-1]

        @pl.when(pl.program_id(0) == 0)
        def _():
            seat = lax.axis_index("tensor")
            for k, part in enumerate(parts):
                cot[pl.ds(pl.multiple_of((seat ^ k) * depth, depth), depth), :] = part[...]

        for j in range(chunks):
            here = slice(j * width, (j + 1) * width)
            acc = jnp.dot(acts_ref[...], cot[:, here], preferred_element_type=F32)
            top[0, :, here] = jnp.max(jnp.abs(acc).reshape(blocks, BLOCK, width), axis=1)
            outs[j][...] = acc.astype(BF16)

    out = pl.pallas_call(
        kernel,
        grid=(rows // step,),
        in_specs=[pl.BlockSpec((step, tokens), lambda i: (i, 0))]
        + [pl.BlockSpec((depth, columns), lambda i: (0, 0))] * len(group),
        out_specs=[pl.BlockSpec((step, width), lambda i: (i, 0))] * chunks
        + [pl.BlockSpec((1, blocks, columns), lambda i: (i, 0, 0))],
        out_shape=[jax.ShapeDtypeStruct((rows, width), BF16)] * chunks
        + [jax.ShapeDtypeStruct((rows // step, blocks, columns), F32)],
        scratch_shapes=[pltpu.VMEM((tokens, columns), BF16)],
        compiler_params=pltpu.CompilerParams(vmem_limit_bytes=48 * 1024 * 1024),
        cost_estimate=cost,
        name="partials",
    )(acts_t, *group)
    return out[:chunks], out[chunks]


def add(terms, *earlier, rows=None):
    held = lax.optimization_barrier((*terms, *earlier))[: len(terms)]
    if rows is not None:
        held = [term if term.shape[0] == rows[1] else lax.slice_in_dim(term, rows[0], sum(rows)) for term in held]
    total = held[0].astype(F32)
    for term in held[1:]:
        total = total + term.astype(F32)
    return lax.optimization_barrier(total.astype(BF16))


def adamw(terms, states, factor):
    total = terms[0].astype(F32)
    for term in terms[1:]:
        total = total + term.astype(F32)
    master, first_moment, second_moment = states
    gradient = total * factor
    new_first = 0.9 * first_moment + 0.1 * gradient
    new_second = 0.95 * second_moment + 0.05 * gradient * gradient
    first_hat = new_first * (1.0 / (1.0 - 0.9**10))
    second_hat = new_second * (1.0 / (1.0 - 0.95**10))
    new_master = master * (1.0 - 0.01 * 0.1) - 0.01 * first_hat / (jnp.sqrt(second_hat) + 1e-08)
    return new_master, new_first, new_second, new_master.astype(BF16)


def update(terms, states, factor, wanted, name):
    rows, width = states[0].shape
    step = min(rows // 2, 512)
    half = rows // 2 // step
    flat = [value for term in terms for value in (term if isinstance(term, tuple) else (term,))]
    dtypes = [(F32, F32, F32, BF16)[k] for k in wanted]

    def kernel(*refs):
        ins, outs = refs[: len(flat) + 3], refs[len(flat) + 3 :]
        values, at = [], 0
        for term in terms:
            if isinstance(term, tuple):
                values.append(jnp.where(pl.program_id(0) < half, ins[at][...], ins[at + 1][...]))
                at += 2
            else:
                values.append(ins[at][...])
                at += 1
        results = adamw(values, [ref[...] for ref in ins[at:]], factor)
        for out, k in zip(outs, wanted):
            out[...] = results[k]

    whole = pl.BlockSpec((step, width), lambda i: (i, 0))
    halves = [
        pl.BlockSpec((step, width), lambda i: (jnp.minimum(i, half - 1), 0)),
        pl.BlockSpec((step, width), lambda i: (jnp.maximum(i - half, 0), 0)),
    ]
    specs = [spec for term in terms for spec in (halves if isinstance(term, tuple) else [whole])]
    return pl.pallas_call(
        kernel,
        grid=(rows // step,),
        in_specs=specs + [whole] * 3,
        out_specs=[whole] * len(wanted),
        out_shape=[jax.ShapeDtypeStruct((rows, width), dtype) for dtype in dtypes],
        compiler_params=pltpu.CompilerParams(vmem_limit_bytes=48 * 1024 * 1024),
        cost_estimate=FREE,
        name=name,
    )(*flat, *states)


def blank(shape, dtype):
    return pl.pallas_call(
        lambda ref: None,
        out_specs=pl.BlockSpec(memory_space=pl.ANY),
        out_shape=jax.ShapeDtypeStruct(shape, dtype),
        cost_estimate=FREE,
        name="blank",
    )()


def after(value, *earlier):
    return lax.optimization_barrier((value, *earlier))[0] if earlier else value


def tie(*values):
    return lax.optimization_barrier(values)


def body(acts, cotangent, master, first_moment, second_moment):
    n_dp = lax.axis_size("dp")
    n_tensor = lax.axis_size("tensor")
    n_x = n_dp // Z
    owner = lax.axis_index("dp")
    z, x = owner // n_x, owner % n_x
    rows, columns = acts.shape[1], cotangent.shape[1]
    width = columns // n_dp
    high = width // BLOCK
    others = range(1, n_x)

    def z_perm(value, pairs):
        return lax.ppermute(value, "dp", [(a * n_x + i, b * n_x + i) for a, b in pairs for i in range(n_x)])

    def x_perm(value, by, where=range(Z)):
        pairs = [(a * n_x + i, a * n_x + (i + by) % n_x) for a in where for i in range(n_x)]
        return lax.ppermute(value, "dp", pairs)

    def seat_perm(value, flip):
        return lax.ppermute(value, "tensor", [(i, i ^ flip) for i in range(n_tensor)])

    pieces = [
        [(0, by) for by in others],
        [(0, 0)] + [(1, by) for by in others],
        [(i, by) for i in (2, 3) for by in others] + [(1, 0), (2, 0), (3, 0)],
    ]
    own = arrange(cotangent, pieces, width, n_x)
    partial, tops, across = {}, [], []

    def fetch(piece, *earlier):
        value = after(own[piece], *earlier)
        across.append([value] + [seat_perm(value, k) for k in range(2, n_tensor, 2)])

    def partials(piece, *earlier):
        group = [part for value in across[piece] for part in (value, seat_perm(after(value, *earlier), 1))]
        cost = FREE if piece else pl.CostEstimate(flops=10**10, bytes_accessed=acts.size, transcendentals=0)
        chunks, top = multiply(after(acts_t, *earlier), group, len(pieces[piece]), width, cost)
        partial.update(zip(pieces[piece], chunks))
        tops.append(top)
        return chunks[0]

    def send_x(slot):
        return [x_perm(partial[slot, by], by) for by in others]

    half = rows // 2
    halves = range(2)
    part = [(h * half, half) for h in halves]

    for piece in range(len(pieces)):
        fetch(piece)
    acts_t = after(acts, *own).T
    token = partials(0, acts_t)
    got0 = send_x(0)
    token = partials(1, token)
    got1 = send_x(1)
    far, middle = [None] * 2, [None] * 2
    for h in halves:
        token = add([partial[0, 0], *got0], token, rows=part[h])
        far[h] = z_perm(token, INWARDS)
    token = partials(2, token)
    got2, got3 = send_x(2), send_x(3)
    token = add([partial[1, 0], *got1], token)
    inwards = z_perm(token, INWARDS)
    for h in halves:
        token = add([partial[0, 0], *got0, far[h]], token, rows=part[h])
        middle[h] = z_perm(token, MIDDLE)

    top = jnp.concatenate([after(t, token).reshape(rows // BLOCK, -1, BLOCK).max(axis=2) for t in tops], axis=1)
    column = jnp.stack(
        [(owner_z(z, i) * n_x + (x + by) % n_x) * high + h for piece in pieces for i, by in piece for h in range(high)]
    )
    here = column[None, :, None] == jnp.arange(n_dp * high)[None, None, :]
    scales = jnp.max(jnp.where(here, top[:, :, None], 0.0), axis=1)
    scales_x = [x_perm(scales, by) for by in others]

    pairs = [None] * 2
    token = add([partial[2, 0], *got2, middle[0]], scales, rows=part[0])
    pairs[0] = z_perm(token, PAIRS)
    token = add([partial[1, 0], *got1, inwards], token)
    last = z_perm(token, MIDDLE)
    token = add([partial[2, 0], *got2, middle[1]], token, pairs[0], rows=part[1])
    pairs[1] = z_perm(token, PAIRS)

    terms = [after(partial[3, 0], *scales_x), *got3, last, tuple(pairs)]
    states = [master, first_moment, second_moment]
    factor = 1.0 / math.sqrt(acts.shape[0] * n_dp)
    owned = []
    for h in halves:
        held = lax.optimization_barrier((*terms[:-1], *states, pairs[h]))
        cut = [lax.slice_in_dim(value, h * half, (h + 1) * half) for value in held[:-1]]
        value = adamw(cut[: len(terms) - 1] + [held[-1]], cut[len(terms) - 1 :], factor)[3]
        owned.append(lax.optimization_barrier(value))
        if h == 0:
            terms[0], owned[0] = tie(terms[0], owned[0])
    terms[0], owned[1] = tie(terms[0], owned[1])
    new_master, new_first, new_second = update(terms, states, factor, [0, 1, 2], "states")

    low, between = z < 2, (z == 1) | (z == 2)
    sources = [z, z ^ 1, jnp.where(low, 2, 1), jnp.where(low, 3, 0)]
    over = [[None] * 2 for _ in range(Z)]
    pairs, mid, mid_far, outwards, near, far, distant = [[None] * 2 for _ in range(7)]

    def over_x(value):
        return [x_perm(value, by) for by in others]

    for h in halves:
        over[0][h] = over_x(owned[h])
        pairs[h], mid[h] = z_perm(owned[h], PAIRS), z_perm(owned[h], MIDDLE)
    for h in halves:
        pairs[h], mid[h], *over[0][h] = tie(pairs[h], mid[h], *over[0][h])
        over[1][h] = over_x(pairs[h])
        mid_far[h], outwards[h] = z_perm(pairs[h], MIDDLE), z_perm(mid[h], OUTWARDS)
    for h in halves:
        mid_far[h], outwards[h], mid[h], *over[1][h] = tie(mid_far[h], outwards[h], mid[h], *over[1][h])
        far[h] = z_perm(mid_far[h], OUTWARDS)
        (near[h],) = tie(jnp.where(between, mid[h], outwards[h]))
        over[2][h] = over_x(near[h])
    for h in halves:
        if h:
            far[h], distant[0] = tie(far[h], distant[0])
        (distant[h],) = tie(jnp.where(between, mid_far[h], far[h]))
        over[3][h] = over_x(distant[h])

    def put(weights, h, slot, by):
        value = [owned, pairs, near, distant][slot][h] if by == 0 else over[slot][h][by - 1]
        at = (sources[slot] * n_x + (x - by) % n_x) * width
        return lax.dynamic_update_slice(weights, value, (h * half, at))

    weights, near[1] = tie(blank((rows, columns), BF16), near[1])
    for slot in range(2):
        for h in halves:
            for by in range(n_x):
                weights = put(weights, h, slot, by)
    weights, distant[1] = tie(weights, distant[1])
    for slot in range(2, Z):
        for h in halves:
            weights = put(weights, h, slot, 0)
    for slot in range(2, Z):
        for h in halves:
            for by in others:
                weights = put(weights, h, slot, by)
    scales, distant[1] = tie(scales, distant[1])
    for got in scales_x:
        scales = jnp.maximum(scales, got)
    scales = jnp.maximum(scales, z_perm(scales, PAIRS))
    scales_z = z_perm(scales, [(a, a ^ 2) for a in range(Z)])
    block_scales = jnp.maximum(scales, scales_z) + 1e-06
    return (new_master, new_first, new_second, weights, block_scales)


def solution(mesh):
    in_specs = (
        P("dp", "tensor"),
        P(("dp", "tensor"), None),
        P("tensor", "dp"),
        P("tensor", "dp"),
        P("tensor", "dp"),
    )
    out_specs = (
        P("tensor", "dp"),
        P("tensor", "dp"),
        P("tensor", "dp"),
        P("tensor", None),
        P("tensor", None),
    )
    return jax.shard_map(body, mesh=mesh, in_specs=in_specs, out_specs=out_specs, check_vma=False)
```

```python
import math

import jax
import jax.numpy as jnp
from jax import lax
from jax.experimental import pallas as pl
from jax.experimental.pallas import tpu as pltpu
from jax.sharding import PartitionSpec as P

BLOCK = 128
Z = 4
F32 = jnp.float32
BF16 = jnp.bfloat16
VMEM = pl.BlockSpec(memory_space=pltpu.VMEM)
FREE = pl.CostEstimate(flops=0, bytes_accessed=0, transcendentals=0)

INWARDS = ((0, 1), (3, 2))
OUTWARDS = ((1, 0), (2, 3))
MIDDLE = ((1, 2), (2, 1))
PAIRS = ((0, 1), (1, 0), (2, 3), (3, 2))


def owner_z(z, slot):
    low = z < 2
    if slot == 3:
        return z
    if slot == 0:
        return jnp.where(low, 3, 0)
    end = (z == 0) | (z == Z - 1)
    two, one = jnp.where(low, 2, 1), jnp.where(end, jnp.where(low, 1, 2), jnp.where(low, 0, 3))
    return two if slot == 1 else one


def call(kernel, out_shape, operands, name):
    return pl.pallas_call(
        kernel,
        out_shape=list(out_shape),
        in_specs=[VMEM] * len(operands),
        out_specs=[VMEM] * len(out_shape),
        cost_estimate=FREE,
        name=name,
    )


def arrange(cot, pieces, width, n_x):
    def kernel(cot_ref, *outs):
        owner = lax.axis_index("dp")
        z, x = owner // n_x, owner % n_x
        for piece, out in zip(pieces, outs):
            for j, (slot, by) in enumerate(piece):
                at = pl.multiple_of((owner_z(z, slot) * n_x + (x + by) % n_x) * width, width)
                out[:, j * width : (j + 1) * width] = cot_ref[:, pl.ds(at, width)]

    shapes = [jax.ShapeDtypeStruct((cot.shape[0], len(piece) * width), BF16) for piece in pieces]
    return call(kernel, shapes, [cot], "arrange")(cot)


def multiply(acts_t, group, chunks, width, cost):
    rows, tokens = acts_t.shape
    depth, columns = group[0].shape
    step = min(rows, 512)
    blocks = step // BLOCK

    def kernel(acts_ref, *refs):
        parts, outs, top, cot = refs[: len(group)], refs[len(group) : -2], refs[-2], refs[-1]

        @pl.when(pl.program_id(0) == 0)
        def _():
            seat = lax.axis_index("tensor")
            for k, part in enumerate(parts):
                cot[pl.ds(pl.multiple_of((seat ^ k) * depth, depth), depth), :] = part[...]

        for j in range(chunks):
            here = slice(j * width, (j + 1) * width)
            acc = jnp.dot(acts_ref[...], cot[:, here], preferred_element_type=F32)
            top[0, :, here] = jnp.max(jnp.abs(acc).reshape(blocks, BLOCK, width), axis=1)
            outs[j][...] = acc.astype(BF16)

    out = pl.pallas_call(
        kernel,
        grid=(rows // step,),
        in_specs=[pl.BlockSpec((step, tokens), lambda i: (i, 0))]
        + [pl.BlockSpec((depth, columns), lambda i: (0, 0))] * len(group),
        out_specs=[pl.BlockSpec((step, width), lambda i: (i, 0))] * chunks
        + [pl.BlockSpec((1, blocks, columns), lambda i: (i, 0, 0))],
        out_shape=[jax.ShapeDtypeStruct((rows, width), BF16)] * chunks
        + [jax.ShapeDtypeStruct((rows // step, blocks, columns), F32)],
        scratch_shapes=[pltpu.VMEM((tokens, columns), BF16)],
        compiler_params=pltpu.CompilerParams(vmem_limit_bytes=48 * 1024 * 1024),
        cost_estimate=cost,
        name="partials",
    )(acts_t, *group)
    return out[:chunks], out[chunks]


def add(terms, *earlier, rows=None):
    held = lax.optimization_barrier((*terms, *earlier))[: len(terms)]
    if rows is not None:
        held = [term if term.shape[0] == rows[1] else lax.slice_in_dim(term, rows[0], sum(rows)) for term in held]
    total = held[0].astype(F32)
    for term in held[1:]:
        total = total + term.astype(F32)
    return lax.optimization_barrier(total.astype(BF16))


def adamw(terms, states, factor):
    total = terms[0].astype(F32)
    for term in terms[1:]:
        total = total + term.astype(F32)
    master, first_moment, second_moment = states
    gradient = total * factor
    new_first = 0.9 * first_moment + 0.1 * gradient
    new_second = 0.95 * second_moment + 0.05 * gradient * gradient
    first_hat = new_first * (1.0 / (1.0 - 0.9**10))
    second_hat = new_second * (1.0 / (1.0 - 0.95**10))
    new_master = master * (1.0 - 0.01 * 0.1) - 0.01 * first_hat / (jnp.sqrt(second_hat) + 1e-08)
    return new_master, new_first, new_second, new_master.astype(BF16)


def update(terms, states, factor, wanted, name, split=False):
    rows, width = states[0].shape
    step = min(rows // 2, 512)
    half = rows // 2 // step
    flat = [value for term in terms for value in (term if isinstance(term, tuple) else (term,))]
    dtypes = [(F32, F32, F32, BF16)[k] for k in wanted]

    def kernel(*refs):
        ins, outs = refs[: len(flat) + 3], refs[len(flat) + 3 :]
        values, at = [], 0
        for term in terms:
            if isinstance(term, tuple):
                values.append(jnp.where(pl.program_id(0) < half, ins[at][...], ins[at + 1][...]))
                at += 2
            else:
                values.append(ins[at][...])
                at += 1
        results = adamw(values, [ref[...] for ref in ins[at:]], factor)
        if split:
            for k, out in enumerate(outs):

                @pl.when(pl.program_id(0) // half == k)
                def _(out=out):
                    out[...] = results[wanted[0]]

        else:
            for out, k in zip(outs, wanted):
                out[...] = results[k]

    whole = pl.BlockSpec((step, width), lambda i: (i, 0))
    halves = [
        pl.BlockSpec((step, width), lambda i: (jnp.minimum(i, half - 1), 0)),
        pl.BlockSpec((step, width), lambda i: (jnp.maximum(i - half, 0), 0)),
    ]
    specs = [spec for term in terms for spec in (halves if isinstance(term, tuple) else [whole])]
    return pl.pallas_call(
        kernel,
        grid=(rows // step,),
        in_specs=specs + [whole] * 3,
        out_specs=halves if split else [whole] * len(wanted),
        out_shape=[jax.ShapeDtypeStruct((rows // 2, width), dtypes[0])] * 2
        if split
        else [jax.ShapeDtypeStruct((rows, width), dtype) for dtype in dtypes],
        compiler_params=pltpu.CompilerParams(vmem_limit_bytes=48 * 1024 * 1024),
        cost_estimate=FREE,
        name=name,
    )(*flat, *states)


def blank(shape, dtype):
    return pl.pallas_call(
        lambda ref: None,
        out_specs=pl.BlockSpec(memory_space=pl.ANY),
        out_shape=jax.ShapeDtypeStruct(shape, dtype),
        cost_estimate=FREE,
        name="blank",
    )()


def after(value, *earlier):
    return lax.optimization_barrier((value, *earlier))[0] if earlier else value


def tie(*values):
    return lax.optimization_barrier(values)


def body(acts, cotangent, master, first_moment, second_moment):
    n_dp = lax.axis_size("dp")
    n_tensor = lax.axis_size("tensor")
    n_x = n_dp // Z
    owner = lax.axis_index("dp")
    z, x = owner // n_x, owner % n_x
    rows, columns = acts.shape[1], cotangent.shape[1]
    width = columns // n_dp
    high = width // BLOCK
    others = range(1, n_x)

    def z_perm(value, pairs):
        return lax.ppermute(value, "dp", [(a * n_x + i, b * n_x + i) for a, b in pairs for i in range(n_x)])

    def x_perm(value, by, where=range(Z)):
        pairs = [(a * n_x + i, a * n_x + (i + by) % n_x) for a in where for i in range(n_x)]
        return lax.ppermute(value, "dp", pairs)

    def seat_perm(value, flip):
        return lax.ppermute(value, "tensor", [(i, i ^ flip) for i in range(n_tensor)])

    pieces = [
        [(0, by) for by in others],
        [(0, 0)] + [(1, by) for by in others],
        [(i, by) for i in (2, 3) for by in others] + [(1, 0), (2, 0), (3, 0)],
    ]
    own = arrange(cotangent, pieces, width, n_x)
    partial, tops, across = {}, [], []

    def fetch(piece, *earlier):
        value = after(own[piece], *earlier)
        across.append([value] + [seat_perm(value, k) for k in range(2, n_tensor, 2)])

    def partials(piece, *earlier):
        group = [part for value in across[piece] for part in (value, seat_perm(after(value, *earlier), 1))]
        cost = FREE if piece else pl.CostEstimate(flops=10**10, bytes_accessed=acts.size, transcendentals=0)
        chunks, top = multiply(after(acts_t, *earlier), group, len(pieces[piece]), width, cost)
        partial.update(zip(pieces[piece], chunks))
        tops.append(top)
        return chunks[0]

    def send_x(slot):
        return [x_perm(partial[slot, by], by) for by in others]

    half = rows // 2
    halves = range(2)
    part = [(h * half, half) for h in halves]

    for piece in range(len(pieces)):
        fetch(piece)
    acts_t = after(acts, *own).T
    token = partials(0, acts_t)
    got0 = send_x(0)
    token = partials(1, token)
    got1 = send_x(1)
    far, middle = [None] * 2, [None] * 2
    for h in halves:
        token = add([partial[0, 0], *got0], token, rows=part[h])
        far[h] = z_perm(token, INWARDS)
    token = partials(2, token)
    got2, got3 = send_x(2), send_x(3)
    token = add([partial[1, 0], *got1], token)
    inwards = z_perm(token, INWARDS)
    for h in halves:
        token = add([partial[0, 0], *got0, far[h]], token, rows=part[h])
        middle[h] = z_perm(token, MIDDLE)

    top = jnp.concatenate([after(t, token).reshape(rows // BLOCK, -1, BLOCK).max(axis=2) for t in tops], axis=1)
    column = jnp.stack(
        [(owner_z(z, i) * n_x + (x + by) % n_x) * high + h for piece in pieces for i, by in piece for h in range(high)]
    )
    here = column[None, :, None] == jnp.arange(n_dp * high)[None, None, :]
    scales = jnp.max(jnp.where(here, top[:, :, None], 0.0), axis=1)
    scales_x = [x_perm(scales, by) for by in others]

    pairs = [None] * 2
    token = add([partial[2, 0], *got2, middle[0]], scales, rows=part[0])
    pairs[0] = z_perm(token, PAIRS)
    token = add([partial[1, 0], *got1, inwards], token)
    last = z_perm(token, MIDDLE)
    token = add([partial[2, 0], *got2, middle[1]], token, pairs[0], rows=part[1])
    pairs[1] = z_perm(token, PAIRS)

    terms = [after(partial[3, 0], *scales_x), *got3, last, tuple(pairs)]
    states = [master, first_moment, second_moment]
    factor = 1.0 / math.sqrt(acts.shape[0] * n_dp)
    owned = update(terms, states, factor, [3], "weights", split=True)
    terms[0], *owned = tie(terms[0], *owned)
    new_master, new_first, new_second = update(terms, states, factor, [0, 1, 2], "states")

    low, between = z < 2, (z == 1) | (z == 2)
    sources = [z, z ^ 1, jnp.where(low, 2, 1), jnp.where(low, 3, 0)]
    over = [[None] * 2 for _ in range(Z)]
    pairs, mid, mid_far, outwards, near, far, distant = [[None] * 2 for _ in range(7)]

    def over_x(value):
        return [x_perm(value, by) for by in others]

    for h in halves:
        over[0][h] = over_x(owned[h])
        pairs[h], mid[h] = z_perm(owned[h], PAIRS), z_perm(owned[h], MIDDLE)
    for h in (1, 0):
        if h == 1:
            pairs[h], mid[h], new_master, *over[0][h] = tie(pairs[h], mid[h], new_master, *over[0][h])
        else:
            pairs[h], mid[h], *over[0][h] = tie(pairs[h], mid[h], *over[0][h])
        over[1][h] = over_x(pairs[h])
        mid_far[h], outwards[h] = z_perm(pairs[h], MIDDLE), z_perm(mid[h], OUTWARDS)
    for h in (0, 1):
        mid_far[h], outwards[h], mid[h], *over[1][h] = tie(mid_far[h], outwards[h], mid[h], *over[1][h])
        far[h] = z_perm(mid_far[h], OUTWARDS)
        (near[h],) = tie(jnp.where(between, mid[h], outwards[h]))
        over[2][h] = over_x(near[h])
    for h in (0, 1):
        (distant[h],) = tie(jnp.where(between, mid_far[h], far[h]))
        over[3][h] = over_x(distant[h])

    def put(weights, h, slot, by):
        value = [owned, pairs, near, distant][slot][h] if by == 0 else over[slot][h][by - 1]
        at = (sources[slot] * n_x + (x - by) % n_x) * width
        return lax.dynamic_update_slice(weights, value, (h * half, at))

    weights, near[1] = tie(blank((rows, columns), BF16), near[1])
    for slot in range(2):
        for h in halves:
            for by in range(n_x):
                weights = put(weights, h, slot, by)
    weights, distant[1] = tie(weights, distant[1])
    for slot in range(2, Z):
        for h in halves:
            weights = put(weights, h, slot, 0)
    for slot in range(2, Z):
        for h in halves:
            for by in others:
                weights = put(weights, h, slot, by)
    scales, distant[1] = tie(scales, distant[1])
    for got in scales_x:
        scales = jnp.maximum(scales, got)
    scales = jnp.maximum(scales, z_perm(scales, PAIRS))
    scales_z = z_perm(scales, [(a, a ^ 2) for a in range(Z)])
    block_scales = jnp.maximum(scales, scales_z) + 1e-06
    return (new_master, new_first, new_second, weights, block_scales)


def solution(mesh):
    in_specs = (
        P("dp", "tensor"),
        P(("dp", "tensor"), None),
        P("tensor", "dp"),
        P("tensor", "dp"),
        P("tensor", "dp"),
    )
    out_specs = (
        P("tensor", "dp"),
        P("tensor", "dp"),
        P("tensor", "dp"),
        P("tensor", None),
        P("tensor", None),
    )
    return jax.shard_map(body, mesh=mesh, in_specs=in_specs, out_specs=out_specs, check_vma=False)
```

```python
import math

import jax
import jax.numpy as jnp
from jax import lax
from jax.experimental import pallas as pl
from jax.experimental.pallas import tpu as pltpu
from jax.sharding import PartitionSpec as P

BLOCK = 128
Z = 4
F32 = jnp.float32
BF16 = jnp.bfloat16
VMEM = pl.BlockSpec(memory_space=pltpu.VMEM)
FREE = pl.CostEstimate(flops=0, bytes_accessed=0, transcendentals=0)

INWARDS = ((0, 1), (3, 2))
OUTWARDS = ((1, 0), (2, 3))
MIDDLE = ((1, 2), (2, 1))
PAIRS = ((0, 1), (1, 0), (2, 3), (3, 2))


def owner_z(z, slot):
    low = z < 2
    if slot == 3:
        return z
    if slot == 0:
        return jnp.where(low, 3, 0)
    end = (z == 0) | (z == Z - 1)
    two, one = jnp.where(low, 2, 1), jnp.where(end, jnp.where(low, 1, 2), jnp.where(low, 0, 3))
    return two if slot == 1 else one


def call(kernel, out_shape, operands, name):
    return pl.pallas_call(
        kernel,
        out_shape=list(out_shape),
        in_specs=[VMEM] * len(operands),
        out_specs=[VMEM] * len(out_shape),
        cost_estimate=FREE,
        name=name,
    )


def arrange(cot, pieces, width, n_x):
    def kernel(cot_ref, *outs):
        owner = lax.axis_index("dp")
        z, x = owner // n_x, owner % n_x
        for piece, out in zip(pieces, outs):
            for j, (slot, by) in enumerate(piece):
                at = pl.multiple_of((owner_z(z, slot) * n_x + (x + by) % n_x) * width, width)
                out[:, j * width : (j + 1) * width] = cot_ref[:, pl.ds(at, width)]

    shapes = [jax.ShapeDtypeStruct((cot.shape[0], len(piece) * width), BF16) for piece in pieces]
    return call(kernel, shapes, [cot], "arrange")(cot)


def multiply(acts_t, group, chunks, width, cost):
    rows, tokens = acts_t.shape
    depth, columns = group[0].shape
    step = min(rows, 512)
    blocks = step // BLOCK

    def kernel(acts_ref, *refs):
        parts, outs, top, cot = refs[: len(group)], refs[len(group) : -2], refs[-2], refs[-1]

        @pl.when(pl.program_id(0) == 0)
        def _():
            seat = lax.axis_index("tensor")
            for k, part in enumerate(parts):
                cot[pl.ds(pl.multiple_of((seat ^ k) * depth, depth), depth), :] = part[...]

        for j in range(chunks):
            here = slice(j * width, (j + 1) * width)
            acc = jnp.dot(acts_ref[...], cot[:, here], preferred_element_type=F32)
            top[0, :, here] = jnp.max(jnp.abs(acc).reshape(blocks, BLOCK, width), axis=1)
            outs[j][...] = acc.astype(BF16)

    out = pl.pallas_call(
        kernel,
        grid=(rows // step,),
        in_specs=[pl.BlockSpec((step, tokens), lambda i: (i, 0))]
        + [pl.BlockSpec((depth, columns), lambda i: (0, 0))] * len(group),
        out_specs=[pl.BlockSpec((step, width), lambda i: (i, 0))] * chunks
        + [pl.BlockSpec((1, blocks, columns), lambda i: (i, 0, 0))],
        out_shape=[jax.ShapeDtypeStruct((rows, width), BF16)] * chunks
        + [jax.ShapeDtypeStruct((rows // step, blocks, columns), F32)],
        scratch_shapes=[pltpu.VMEM((tokens, columns), BF16)],
        compiler_params=pltpu.CompilerParams(vmem_limit_bytes=48 * 1024 * 1024),
        cost_estimate=cost,
        name="partials",
    )(acts_t, *group)
    return out[:chunks], out[chunks]


def add(terms, *earlier, rows=None):
    held = lax.optimization_barrier((*terms, *earlier))[: len(terms)]
    if rows is not None:
        held = [term if term.shape[0] == rows[1] else lax.slice_in_dim(term, rows[0], sum(rows)) for term in held]
    total = held[0].astype(F32)
    for term in held[1:]:
        total = total + term.astype(F32)
    return lax.optimization_barrier(total.astype(BF16))


def adamw(terms, states, factor):
    total = terms[0].astype(F32)
    for term in terms[1:]:
        total = total + term.astype(F32)
    master, first_moment, second_moment = states
    gradient = total * factor
    new_first = 0.9 * first_moment + 0.1 * gradient
    new_second = 0.95 * second_moment + 0.05 * gradient * gradient
    first_hat = new_first * (1.0 / (1.0 - 0.9**10))
    second_hat = new_second * (1.0 / (1.0 - 0.95**10))
    new_master = master * (1.0 - 0.01 * 0.1) - 0.01 * first_hat / (jnp.sqrt(second_hat) + 1e-08)
    return new_master, new_first, new_second, new_master.astype(BF16)


def update(terms, states, factor, wanted, name, split=False):
    rows, width = states[0].shape
    step = min(rows // 2, 512)
    half = rows // 2 // step
    flat = [value for term in terms for value in (term if isinstance(term, tuple) else (term,))]
    dtypes = [(F32, F32, F32, BF16)[k] for k in wanted]

    def kernel(*refs):
        ins, outs = refs[: len(flat) + 3], refs[len(flat) + 3 :]
        values, at = [], 0
        for term in terms:
            if isinstance(term, tuple):
                values.append(jnp.where(pl.program_id(0) < half, ins[at][...], ins[at + 1][...]))
                at += 2
            else:
                values.append(ins[at][...])
                at += 1
        results = adamw(values, [ref[...] for ref in ins[at:]], factor)
        if split:
            for k, out in enumerate(outs):

                @pl.when(pl.program_id(0) // half == k)
                def _(out=out):
                    out[...] = results[wanted[0]]

        else:
            for out, k in zip(outs, wanted):
                out[...] = results[k]

    whole = pl.BlockSpec((step, width), lambda i: (i, 0))
    halves = [
        pl.BlockSpec((step, width), lambda i: (jnp.minimum(i, half - 1), 0)),
        pl.BlockSpec((step, width), lambda i: (jnp.maximum(i - half, 0), 0)),
    ]
    specs = [spec for term in terms for spec in (halves if isinstance(term, tuple) else [whole])]
    return pl.pallas_call(
        kernel,
        grid=(rows // step,),
        in_specs=specs + [whole] * 3,
        out_specs=halves if split else [whole] * len(wanted),
        out_shape=[jax.ShapeDtypeStruct((rows // 2, width), dtypes[0])] * 2
        if split
        else [jax.ShapeDtypeStruct((rows, width), dtype) for dtype in dtypes],
        compiler_params=pltpu.CompilerParams(vmem_limit_bytes=48 * 1024 * 1024),
        cost_estimate=FREE,
        name=name,
    )(*flat, *states)


def blank(shape, dtype):
    return pl.pallas_call(
        lambda ref: None,
        out_specs=pl.BlockSpec(memory_space=pl.ANY),
        out_shape=jax.ShapeDtypeStruct(shape, dtype),
        cost_estimate=FREE,
        name="blank",
    )()


def after(value, *earlier):
    return lax.optimization_barrier((value, *earlier))[0] if earlier else value


def tie(*values):
    return lax.optimization_barrier(values)


def body(acts, cotangent, master, first_moment, second_moment):
    n_dp = lax.axis_size("dp")
    n_tensor = lax.axis_size("tensor")
    n_x = n_dp // Z
    owner = lax.axis_index("dp")
    z, x = owner // n_x, owner % n_x
    rows, columns = acts.shape[1], cotangent.shape[1]
    width = columns // n_dp
    high = width // BLOCK
    others = range(1, n_x)

    def z_perm(value, pairs):
        return lax.ppermute(value, "dp", [(a * n_x + i, b * n_x + i) for a, b in pairs for i in range(n_x)])

    def x_perm(value, by, where=range(Z)):
        pairs = [(a * n_x + i, a * n_x + (i + by) % n_x) for a in where for i in range(n_x)]
        return lax.ppermute(value, "dp", pairs)

    def seat_perm(value, flip):
        return lax.ppermute(value, "tensor", [(i, i ^ flip) for i in range(n_tensor)])

    pieces = [
        [(0, by) for by in others],
        [(0, 0)] + [(1, by) for by in others],
        [(i, by) for i in (2, 3) for by in others] + [(1, 0), (2, 0), (3, 0)],
    ]
    own = arrange(cotangent, pieces, width, n_x)
    partial, tops, across = {}, [], []

    def fetch(piece, *earlier):
        value = after(own[piece], *earlier)
        across.append([value] + [seat_perm(value, k) for k in range(2, n_tensor, 2)])

    def partials(piece, *earlier):
        group = [part for value in across[piece] for part in (value, seat_perm(after(value, *earlier), 1))]
        cost = FREE if piece else pl.CostEstimate(flops=10**10, bytes_accessed=acts.size, transcendentals=0)
        chunks, top = multiply(after(acts_t, *earlier), group, len(pieces[piece]), width, cost)
        partial.update(zip(pieces[piece], chunks))
        tops.append(top)
        return chunks[0]

    def send_x(slot):
        return [x_perm(partial[slot, by], by) for by in others]

    half = rows // 2
    halves = range(2)
    part = [(h * half, half) for h in halves]

    for piece in range(len(pieces)):
        fetch(piece)
    acts_t = after(acts, *own).T
    token = partials(0, acts_t)
    got0 = send_x(0)
    token = partials(1, token)
    got1 = send_x(1)
    far, middle = [None] * 2, [None] * 2
    for h in halves:
        token = add([partial[0, 0], *got0], token, rows=part[h])
        far[h] = z_perm(token, INWARDS)
    token = partials(2, token)
    got2, got3 = send_x(2), send_x(3)
    token = add([partial[1, 0], *got1], token)
    inwards = z_perm(token, INWARDS)
    for h in halves:
        token = add([partial[0, 0], *got0, far[h]], token, rows=part[h])
        middle[h] = z_perm(token, MIDDLE)

    top = jnp.concatenate([after(t, token).reshape(rows // BLOCK, -1, BLOCK).max(axis=2) for t in tops], axis=1)
    column = jnp.stack(
        [(owner_z(z, i) * n_x + (x + by) % n_x) * high + h for piece in pieces for i, by in piece for h in range(high)]
    )
    here = column[None, :, None] == jnp.arange(n_dp * high)[None, None, :]
    scales = jnp.max(jnp.where(here, top[:, :, None], 0.0), axis=1)
    scales_x = [x_perm(scales, by) for by in others]

    pairs = [None] * 2
    token = add([partial[2, 0], *got2, middle[0]], scales, rows=part[0])
    pairs[0] = z_perm(token, PAIRS)
    token = add([partial[1, 0], *got1, inwards], token)
    last = z_perm(token, MIDDLE)
    token = add([partial[2, 0], *got2, middle[1]], token, pairs[0], rows=part[1])
    pairs[1] = z_perm(token, PAIRS)

    terms = [after(partial[3, 0], *scales_x), *got3, last, tuple(pairs)]
    states = [master, first_moment, second_moment]
    factor = 1.0 / math.sqrt(acts.shape[0] * n_dp)
    owned = update(terms, states, factor, [3], "weights", split=True)
    terms[0], *owned = tie(terms[0], *owned)
    new_master, new_first, new_second = update(terms, states, factor, [0, 1, 2], "states")

    low, between = z < 2, (z == 1) | (z == 2)
    sources = [z, z ^ 1, jnp.where(low, 2, 1), jnp.where(low, 3, 0)]
    over = [[None] * 2 for _ in range(Z)]
    pairs, mid, mid_far, outwards, near, far, distant = [[None] * 2 for _ in range(7)]

    def over_x(value):
        return [x_perm(value, by) for by in others]

    for h in halves:
        over[0][h] = over_x(owned[h])
        pairs[h], mid[h] = z_perm(owned[h], PAIRS), z_perm(owned[h], MIDDLE)
    def put(weights, h, slot, by, count=half):
        value = [owned, pairs, near, distant][slot][h] if by == 0 else over[slot][h][by - 1]
        at = (sources[slot] * n_x + (x - by) % n_x) * width
        return lax.dynamic_update_slice(weights, value[:count], (h * half, at))

    weights = blank((rows, columns), BF16)
    for h in (1,):
        weights = put(weights, h, 0, 1, 16)
    for h in (1, 0):
        if h == 1:
            pairs[h], mid[h], weights = tie(pairs[h], mid[h], weights)
        else:
            pairs[h], mid[h], new_master, *over[0][h] = tie(pairs[h], mid[h], new_master, *over[0][h])
        over[1][h] = over_x(pairs[h])
        mid_far[h], outwards[h] = z_perm(pairs[h], MIDDLE), z_perm(mid[h], OUTWARDS)
    for h in (0, 1):
        mid_far[h], outwards[h], mid[h], *over[1][h] = tie(mid_far[h], outwards[h], mid[h], *over[1][h])
        far[h] = z_perm(mid_far[h], OUTWARDS)
        (near[h],) = tie(jnp.where(between, mid[h], outwards[h]))
        over[2][h] = over_x(near[h])
    for h in (0, 1):
        (distant[h],) = tie(jnp.where(between, mid_far[h], far[h]))
        over[3][h] = over_x(distant[h])

    weights, near[1] = tie(weights, near[1])
    for slot in range(2):
        for h in halves:
            for by in range(n_x):
                weights = put(weights, h, slot, by)
    weights, distant[1] = tie(weights, distant[1])
    for slot in range(2, Z):
        for h in halves:
            weights = put(weights, h, slot, 0)
    for slot in range(2, Z):
        for h in halves:
            for by in others:
                weights = put(weights, h, slot, by)
    scales, distant[1] = tie(scales, distant[1])
    for got in scales_x:
        scales = jnp.maximum(scales, got)
    scales = jnp.maximum(scales, z_perm(scales, PAIRS))
    scales_z = z_perm(scales, [(a, a ^ 2) for a in range(Z)])
    block_scales = jnp.maximum(scales, scales_z) + 1e-06
    return (new_master, new_first, new_second, weights, block_scales)


def solution(mesh):
    in_specs = (
        P("dp", "tensor"),
        P(("dp", "tensor"), None),
        P("tensor", "dp"),
        P("tensor", "dp"),
        P("tensor", "dp"),
    )
    out_specs = (
        P("tensor", "dp"),
        P("tensor", "dp"),
        P("tensor", "dp"),
        P("tensor", None),
        P("tensor", None),
    )
    return jax.shard_map(body, mesh=mesh, in_specs=in_specs, out_specs=out_specs, check_vma=False)
```

```python
import math

import jax
import jax.numpy as jnp
from jax import lax
from jax.experimental import pallas as pl
from jax.experimental.pallas import tpu as pltpu
from jax.sharding import PartitionSpec as P

BLOCK = 128
Z = 4
F32 = jnp.float32
BF16 = jnp.bfloat16
VMEM = pl.BlockSpec(memory_space=pltpu.VMEM)
FREE = pl.CostEstimate(flops=0, bytes_accessed=0, transcendentals=0)

INWARDS = ((0, 1), (3, 2))
OUTWARDS = ((1, 0), (2, 3))
MIDDLE = ((1, 2), (2, 1))
PAIRS = ((0, 1), (1, 0), (2, 3), (3, 2))


def owner_z(z, slot):
    low = z < 2
    if slot == 3:
        return z
    if slot == 0:
        return jnp.where(low, 3, 0)
    end = (z == 0) | (z == Z - 1)
    two, one = jnp.where(low, 2, 1), jnp.where(end, jnp.where(low, 1, 2), jnp.where(low, 0, 3))
    return two if slot == 1 else one


def call(kernel, out_shape, operands, name):
    return pl.pallas_call(
        kernel,
        out_shape=list(out_shape),
        in_specs=[VMEM] * len(operands),
        out_specs=[VMEM] * len(out_shape),
        cost_estimate=FREE,
        name=name,
    )


def arrange(cot, pieces, width, n_x):
    def kernel(cot_ref, *outs):
        owner = lax.axis_index("dp")
        z, x = owner // n_x, owner % n_x
        for piece, out in zip(pieces, outs):
            for j, (slot, by) in enumerate(piece):
                at = pl.multiple_of((owner_z(z, slot) * n_x + (x + by) % n_x) * width, width)
                out[:, j * width : (j + 1) * width] = cot_ref[:, pl.ds(at, width)]

    shapes = [jax.ShapeDtypeStruct((cot.shape[0], len(piece) * width), BF16) for piece in pieces]
    return call(kernel, shapes, [cot], "arrange")(cot)


def multiply(acts_t, group, chunks, width, cost):
    rows, tokens = acts_t.shape
    depth, columns = group[0].shape
    step = min(rows, 512)
    blocks = step // BLOCK

    def kernel(acts_ref, *refs):
        parts, outs, top, cot = refs[: len(group)], refs[len(group) : -2], refs[-2], refs[-1]

        @pl.when(pl.program_id(0) == 0)
        def _():
            seat = lax.axis_index("tensor")
            for k, part in enumerate(parts):
                cot[pl.ds(pl.multiple_of((seat ^ k) * depth, depth), depth), :] = part[...]

        for j in range(chunks):
            here = slice(j * width, (j + 1) * width)
            acc = jnp.dot(acts_ref[...], cot[:, here], preferred_element_type=F32)
            top[0, :, here] = jnp.max(jnp.abs(acc).reshape(blocks, BLOCK, width), axis=1)
            outs[j][...] = acc.astype(BF16)

    out = pl.pallas_call(
        kernel,
        grid=(rows // step,),
        in_specs=[pl.BlockSpec((step, tokens), lambda i: (i, 0))]
        + [pl.BlockSpec((depth, columns), lambda i: (0, 0))] * len(group),
        out_specs=[pl.BlockSpec((step, width), lambda i: (i, 0))] * chunks
        + [pl.BlockSpec((1, blocks, columns), lambda i: (i, 0, 0))],
        out_shape=[jax.ShapeDtypeStruct((rows, width), BF16)] * chunks
        + [jax.ShapeDtypeStruct((rows // step, blocks, columns), F32)],
        scratch_shapes=[pltpu.VMEM((tokens, columns), BF16)],
        compiler_params=pltpu.CompilerParams(vmem_limit_bytes=48 * 1024 * 1024),
        cost_estimate=cost,
        name="partials",
    )(acts_t, *group)
    return out[:chunks], out[chunks]


def add(terms, *earlier, rows=None):
    held = lax.optimization_barrier((*terms, *earlier))[: len(terms)]
    if rows is not None:
        held = [term if term.shape[0] == rows[1] else lax.slice_in_dim(term, rows[0], sum(rows)) for term in held]
    total = held[0].astype(F32)
    for term in held[1:]:
        total = total + term.astype(F32)
    return lax.optimization_barrier(total.astype(BF16))


def adamw(terms, states, factor):
    total = terms[0].astype(F32)
    for term in terms[1:]:
        total = total + term.astype(F32)
    master, first_moment, second_moment = states
    gradient = total * factor
    new_first = 0.9 * first_moment + 0.1 * gradient
    new_second = 0.95 * second_moment + 0.05 * gradient * gradient
    first_hat = new_first * (1.0 / (1.0 - 0.9**10))
    second_hat = new_second * (1.0 / (1.0 - 0.95**10))
    new_master = master * (1.0 - 0.01 * 0.1) - 0.01 * first_hat / (jnp.sqrt(second_hat) + 1e-08)
    return new_master, new_first, new_second, new_master.astype(BF16)


def update(terms, states, factor, wanted, name, split=False):
    rows, width = states[0].shape
    step = min(rows // 2, 512)
    half = rows // 2 // step
    flat = [value for term in terms for value in (term if isinstance(term, tuple) else (term,))]
    dtypes = [(F32, F32, F32, BF16)[k] for k in wanted]

    def kernel(*refs):
        ins, outs = refs[: len(flat) + 3], refs[len(flat) + 3 :]
        values, at = [], 0
        for term in terms:
            if isinstance(term, tuple):
                values.append(jnp.where(pl.program_id(0) < half, ins[at][...], ins[at + 1][...]))
                at += 2
            else:
                values.append(ins[at][...])
                at += 1
        results = adamw(values, [ref[...] for ref in ins[at:]], factor)
        if split:
            for k, out in enumerate(outs):

                @pl.when(pl.program_id(0) // half == k)
                def _(out=out):
                    out[...] = results[wanted[0]]

        else:
            for out, k in zip(outs, wanted):
                out[...] = results[k]

    whole = pl.BlockSpec((step, width), lambda i: (i, 0))
    halves = [
        pl.BlockSpec((step, width), lambda i: (jnp.minimum(i, half - 1), 0)),
        pl.BlockSpec((step, width), lambda i: (jnp.maximum(i - half, 0), 0)),
    ]
    specs = [spec for term in terms for spec in (halves if isinstance(term, tuple) else [whole])]
    return pl.pallas_call(
        kernel,
        grid=(rows // step,),
        in_specs=specs + [whole] * 3,
        out_specs=halves if split else [whole] * len(wanted),
        out_shape=[jax.ShapeDtypeStruct((rows // 2, width), dtypes[0])] * 2
        if split
        else [jax.ShapeDtypeStruct((rows, width), dtype) for dtype in dtypes],
        compiler_params=pltpu.CompilerParams(vmem_limit_bytes=48 * 1024 * 1024),
        cost_estimate=FREE,
        name=name,
    )(*flat, *states)


def blank(shape, dtype):
    return pl.pallas_call(
        lambda ref: None,
        out_specs=pl.BlockSpec(memory_space=pl.ANY),
        out_shape=jax.ShapeDtypeStruct(shape, dtype),
        cost_estimate=FREE,
        name="blank",
    )()


def after(value, *earlier):
    return lax.optimization_barrier((value, *earlier))[0] if earlier else value


def tie(*values):
    return lax.optimization_barrier(values)


def body(acts, cotangent, master, first_moment, second_moment):
    n_dp = lax.axis_size("dp")
    n_tensor = lax.axis_size("tensor")
    n_x = n_dp // Z
    owner = lax.axis_index("dp")
    z, x = owner // n_x, owner % n_x
    rows, columns = acts.shape[1], cotangent.shape[1]
    width = columns // n_dp
    high = width // BLOCK
    others = range(1, n_x)

    def z_perm(value, pairs):
        return lax.ppermute(value, "dp", [(a * n_x + i, b * n_x + i) for a, b in pairs for i in range(n_x)])

    def x_perm(value, by, where=range(Z)):
        pairs = [(a * n_x + i, a * n_x + (i + by) % n_x) for a in where for i in range(n_x)]
        return lax.ppermute(value, "dp", pairs)

    def seat_perm(value, flip):
        return lax.ppermute(value, "tensor", [(i, i ^ flip) for i in range(n_tensor)])

    pieces = [
        [(0, by) for by in others],
        [(0, 0)] + [(1, by) for by in others],
        [(i, by) for i in (2, 3) for by in others] + [(1, 0), (2, 0), (3, 0)],
    ]
    own = arrange(cotangent, pieces, width, n_x)
    partial, tops, across = {}, [], []

    def fetch(piece, *earlier):
        value = after(own[piece], *earlier)
        across.append([value] + [seat_perm(value, k) for k in range(2, n_tensor, 2)])

    def partials(piece, *earlier):
        group = [part for value in across[piece] for part in (value, seat_perm(after(value, *earlier), 1))]
        cost = FREE if piece else pl.CostEstimate(flops=10**10, bytes_accessed=acts.size, transcendentals=0)
        chunks, top = multiply(after(acts_t, *earlier), group, len(pieces[piece]), width, cost)
        partial.update(zip(pieces[piece], chunks))
        tops.append(top)
        return chunks[0]

    def send_x(slot):
        return [x_perm(partial[slot, by], by) for by in others]

    half = rows // 2
    halves = range(2)
    part = [(h * half, half) for h in halves]

    for piece in range(len(pieces)):
        fetch(piece)
    acts_t = after(acts, *own).T
    token = partials(0, acts_t)
    got0 = send_x(0)
    token = partials(1, token)
    got1 = send_x(1)
    far, middle = [None] * 2, [None] * 2
    for h in halves:
        token = add([partial[0, 0], *got0], token, rows=part[h])
        far[h] = z_perm(token, INWARDS)
    token = partials(2, token)
    got2, got3 = send_x(2), send_x(3)
    token = add([partial[1, 0], *got1], token)
    inwards = z_perm(token, INWARDS)
    for h in halves:
        token = add([partial[0, 0], *got0, far[h]], token, rows=part[h])
        middle[h] = z_perm(token, MIDDLE)

    top = jnp.concatenate([after(t, token).reshape(rows // BLOCK, -1, BLOCK).max(axis=2) for t in tops], axis=1)
    column = jnp.stack(
        [(owner_z(z, i) * n_x + (x + by) % n_x) * high + h for piece in pieces for i, by in piece for h in range(high)]
    )
    here = column[None, :, None] == jnp.arange(n_dp * high)[None, None, :]
    scales = jnp.max(jnp.where(here, top[:, :, None], 0.0), axis=1)
    scales_x = [x_perm(scales, by) for by in others]

    pairs = [None] * 2
    token = add([partial[2, 0], *got2, middle[0]], scales, rows=part[0])
    pairs[0] = z_perm(token, PAIRS)
    token = add([partial[1, 0], *got1, inwards], token)
    last = z_perm(token, MIDDLE)
    token = add([partial[2, 0], *got2, middle[1]], token, pairs[0], rows=part[1])
    pairs[1] = z_perm(token, PAIRS)

    terms = [after(partial[3, 0], *scales_x), *got3, last, tuple(pairs)]
    states = [master, first_moment, second_moment]
    factor = 1.0 / math.sqrt(acts.shape[0] * n_dp)
    owned = update(terms, states, factor, [3], "weights", split=True)
    terms[0], *owned = tie(terms[0], *owned)
    new_master, new_first, new_second = update(terms, states, factor, [0, 1, 2], "states")

    low, between = z < 2, (z == 1) | (z == 2)
    sources = [z, z ^ 1, jnp.where(low, 2, 1), jnp.where(low, 3, 0)]
    over = [[None] * 2 for _ in range(Z)]
    pairs, mid, mid_far, outwards, near, far, distant = [[None] * 2 for _ in range(7)]

    def over_x(value):
        return [x_perm(value, by) for by in others]

    for h in halves:
        over[0][h] = over_x(owned[h])
        pairs[h], mid[h] = z_perm(owned[h], PAIRS), z_perm(owned[h], MIDDLE)
    def put(weights, h, slot, by, count=half):
        value = [owned, pairs, near, distant][slot][h] if by == 0 else over[slot][h][by - 1]
        at = (sources[slot] * n_x + (x - by) % n_x) * width
        return lax.dynamic_update_slice(weights, value[:count], (h * half, at))

    weights = blank((rows, columns), BF16)
    for h in (1,):
        weights = put(weights, h, 0, 1, 16)
    for h in (1, 0):
        if h == 1:
            pairs[h], mid[h], weights = tie(pairs[h], mid[h], weights)
        else:
            pairs[h], mid[h], *over[0][h] = tie(pairs[h], mid[h], *over[0][h])
        over[1][h] = over_x(pairs[h])
        mid_far[h], outwards[h] = z_perm(pairs[h], MIDDLE), z_perm(mid[h], OUTWARDS)
    for h in (0, 1):
        mid_far[h], outwards[h], mid[h], *over[1][h] = tie(mid_far[h], outwards[h], mid[h], *over[1][h])
        far[h] = z_perm(mid_far[h], OUTWARDS)
        near[h], new_master = tie(jnp.where(between, mid[h], outwards[h]), new_master)
        over[2][h] = over_x(near[h])
    for h in (0, 1):
        (distant[h],) = tie(jnp.where(between, mid_far[h], far[h]))
        over[3][h] = over_x(distant[h])

    weights, near[1] = tie(weights, near[1])
    for slot in range(2):
        for h in halves:
            for by in range(n_x):
                weights = put(weights, h, slot, by)
    weights, distant[1] = tie(weights, distant[1])
    for slot in range(2, Z):
        for h in halves:
            weights = put(weights, h, slot, 0)
    for slot in range(2, Z):
        for h in halves:
            for by in others:
                weights = put(weights, h, slot, by)
    scales, distant[1] = tie(scales, distant[1])
    for got in scales_x:
        scales = jnp.maximum(scales, got)
    scales = jnp.maximum(scales, z_perm(scales, PAIRS))
    scales_z = z_perm(scales, [(a, a ^ 2) for a in range(Z)])
    block_scales = jnp.maximum(scales, scales_z) + 1e-06
    return (new_master, new_first, new_second, weights, block_scales)


def solution(mesh):
    in_specs = (
        P("dp", "tensor"),
        P(("dp", "tensor"), None),
        P("tensor", "dp"),
        P("tensor", "dp"),
        P("tensor", "dp"),
    )
    out_specs = (
        P("tensor", "dp"),
        P("tensor", "dp"),
        P("tensor", "dp"),
        P("tensor", None),
        P("tensor", None),
    )
    return jax.shard_map(body, mesh=mesh, in_specs=in_specs, out_specs=out_specs, check_vma=False)
```
